256 devices in a mesh: ctx: 32 (over z_lo, x, core), tp: 8 (over y, z_hi).
Axes of the slice: x: 4, y: 4, z: 8 (z_hi: 2, z_lo: 4; z = z_hi * 4 + z_lo), core: 2. Of those that a mesh axis runs over, the one named last changes fastest.
Arguments:
- query_feat: bfloat16 [8192, 24576], P('tp', 'ctx'), may hold values from -6 to 6
- key_feat: bfloat16 [8192, 24576], P('tp', 'ctx'), may hold values from -6 to 6
- value_feat: bfloat16 [8192, 24576], P('tp', 'ctx'), may hold values from -6 to 6
- grad_out: bfloat16 [8192, 24576], P('tp', 'ctx'), may hold values from -6 to 6
- short_taps: float32 [3, 3, 8192], P(None, None, 'tp'), may hold values from -3 to 3
- filters: bfloat16 [512, 128], P(('tp', 'ctx')), may hold values from -0.48 to 0.48
- skip_bias: bfloat16 [8192], P(('tp', 'ctx')), may hold values from 0.5 to 1.5
Outputs:
- grad_query: bfloat16 [8192, 24576], P('tp', 'ctx')
- grad_key: bfloat16 [8192, 24576], P('tp', 'ctx')
- grad_value: bfloat16 [8192, 24576], P('tp', 'ctx')
- grad_short: float32 [3, 3, 8192], P(None, None, 'tp')
- grad_filters: float32 [512, 128], P(('tp', 'ctx'))
- grad_bias: float32 [8192], P(('tp', 'ctx'))
The draws below stay inside these ranges and needn't reach their ends.
All inputs are finite; a program needn't handle non-finite values.
Results may differ from the reference program's by a relative error of at most 0.019.
Values may be sent and summed in bfloat16 or wider, within the bound.
A program may use at most 192 MiB of HBM per device.

```python
import math
import jax
import jax.numpy as jnp
import numpy as np
from jax import lax

D = 8192
TAPS = 128
GROUP = 16
SHORT = 3
LEN = 24576


def draw_filters(key, part):
    key = jax.random.fold_in(key, 11)
    key_rate, key_tap = jax.random.split(key, 2)
    groups = D // GROUP
    rate = jnp.exp(jax.random.uniform(key_rate, (groups, 1), jnp.float32, math.log(1.0 / 400.0), math.log(1.0 / 20.0)))
    position = jnp.arange(TAPS, dtype=jnp.float32)[None, :]
    raw_taps = jnp.clip(jax.random.normal(key_tap, (groups, TAPS), jnp.float32), -4.0, 4.0)
    return (0.12 * raw_taps * jnp.exp(-rate * position)).astype(jnp.bfloat16)


def block_levels(own_key, dims, shards, low, top_value):
    level, own = 1.0, jax.random.fold_in(own_key, 6)
    for dim, shards_of in shards:
        steps = jnp.exp(jax.random.uniform(jax.random.fold_in(own, dim), (shards_of,), jnp.float32, low / len(shards), top_value / len(shards)))
        level = level * jnp.repeat(steps, dims[dim] // shards_of).reshape([-1 if axis == dim else 1 for axis in range(len(dims))])
    return level


def normal_values(own_key, dims, scale, limit, cuts=(), kind=jnp.bfloat16):
    factor_of = block_levels(own_key, dims, cuts, -0.22, 0.18) if cuts else 1.0
    array = jax.random.normal(own_key, dims, jnp.float32) * scale * factor_of
    return jnp.minimum(jnp.maximum(array, -limit), limit).astype(kind)


def setup_inputs(seed: int = 0) -> dict:
    keys = jax.random.split(jax.random.key(seed), 8)
    return {
        "query_feat": normal_values(keys[0], (D, LEN), 1.0, 6.0, ((0, 8), (1, 32))),
        "key_feat": normal_values(keys[1], (D, LEN), 1.0, 6.0, ((0, 8), (1, 32))),
        "value_feat": normal_values(keys[2], (D, LEN), 1.0, 6.0, ((0, 8), (1, 32))),
        "grad_out": normal_values(keys[3], (D, LEN), 1.0, 6.0, ((0, 8), (1, 32))),
        "short_taps": normal_values(keys[4], (SHORT, SHORT, D), 0.6, 3.0, ((2, 8),), jnp.float32),
        "filters": draw_filters(jax.random.fold_in(keys[7], 71), 0),
        "skip_bias": jnp.clip(0.5 + 1.0 * jax.random.uniform(keys[6], (D,), jnp.float32) ** block_levels(keys[6], (D,), ((0, 256),), -0.2, 0.2), 0.5, 1.5).astype(jnp.bfloat16),
    }


channel_block = 512


def toeplitz(filt):
    rows = np.arange(2 * TAPS)[:, None]
    cols = np.arange(TAPS)[None, :]
    offset = cols - rows + TAPS
    valid = (offset >= 0) & (offset < TAPS)
    picked = jnp.take(filt, np.clip(offset, 0, TAPS - 1).reshape(-1), axis=1)
    picked = picked.reshape(filt.shape[0], 2 * TAPS, TAPS)
    return jnp.where(valid[None], picked, jnp.zeros((), filt.dtype))


def diagonal_sums(difference_matrix):
    groups = difference_matrix.shape[0]
    flipped = difference_matrix[:, ::-1, :]
    padded = jnp.pad(flipped, ((0, 0), (0, 0), (0, 2 * TAPS)))
    skewed = padded.reshape(groups, -1)[:, : 2 * TAPS * (3 * TAPS - 1)]
    skewed = skewed.reshape(groups, 2 * TAPS, 3 * TAPS - 1)
    totals = jnp.sum(skewed, axis=1)
    return totals[:, TAPS - 1: 2 * TAPS - 1]


def short_forward(signal, rim, taps):
    length = signal.shape[1]
    lengthened_input = jnp.concatenate([rim, signal], 1)
    total = jnp.zeros(signal.shape, jnp.float32)
    for offset in range(SHORT):
        start = SHORT - 1 - offset
        total = total + taps[offset][:, None] * lengthened_input[:, start: start + length].astype(jnp.float32)
    return total.astype(jnp.bfloat16), lengthened_input


def short_backward(grad, rim_next, taps, lengthened_input):
    length = grad.shape[1]
    ext_grad = jnp.concatenate([grad, rim_next], 1)
    total = jnp.zeros(grad.shape, jnp.float32)
    tap_terms = []
    for offset in range(SHORT):
        total = total + taps[offset][:, None] * ext_grad[:, offset: offset + length].astype(jnp.float32)
        start = SHORT - 1 - offset
        tap_terms.append(jnp.sum(grad.astype(jnp.float32) * lengthened_input[:, start: start + length].astype(jnp.float32), axis=1))
    return total.astype(jnp.bfloat16), jnp.stack(tap_terms)


def mix_forward(query_conv, product, grad_out, filter_matrix, bias, before):
    channels, length = product.shape
    groups = filter_matrix.shape[0]
    blocks = length // TAPS
    reshaped_rows = product.reshape(groups, channels // groups, blocks, TAPS)
    prior = jnp.concatenate([before.reshape(groups, channels // groups, 1, TAPS), reshaped_rows[:, :, :-1]], 2)
    stacked_rows = jnp.concatenate([prior, reshaped_rows], 3)
    causal_filtering = jnp.einsum('qpxy,qyf->qpxf', stacked_rows.astype(jnp.float32), filter_matrix.astype(jnp.float32))
    bias_col = bias.astype(jnp.float32)[:, None]
    mixed = causal_filtering.reshape(channels, length) + bias_col * product.astype(jnp.float32)
    grad_mixed = (grad_out.astype(jnp.float32) * query_conv.astype(jnp.float32)).astype(jnp.bfloat16)
    grad_qconv = (grad_out.astype(jnp.float32) * mixed).astype(jnp.bfloat16)
    return stacked_rows, grad_mixed, grad_qconv


def mix_backward(stacked_rows, product, grad_mixed, filter_matrix, bias, after):
    channels, length = product.shape
    groups = filter_matrix.shape[0]
    blocks = length // TAPS
    reshaped_rows = grad_mixed.reshape(groups, channels // groups, blocks, TAPS)
    lengthened_input = jnp.concatenate([reshaped_rows, after.reshape(groups, channels // groups, 1, TAPS)], 2)
    reverse_pass = jnp.einsum('hxvp,hop->hxvo', lengthened_input.astype(jnp.float32), filter_matrix.astype(jnp.float32))
    bias_col = bias.astype(jnp.float32)[:, None]
    conv_grad = (reverse_pass[:, :, :-1, TAPS:] + reverse_pass[:, :, 1:, :TAPS]).reshape(channels, length)
    grad_product = (conv_grad + bias_col * grad_mixed.astype(jnp.float32)).astype(jnp.bfloat16)
    difference_matrix = jnp.einsum('finp,finl->fpl', stacked_rows.astype(jnp.float32), reshaped_rows.astype(jnp.float32))
    bias_grad = jnp.sum(grad_mixed.astype(jnp.float32) * product.astype(jnp.float32), axis=1)
    return grad_product, diagonal_sums(difference_matrix), bias_grad


def one_block(pieces):
    query_feat, key_feat, value_feat, grad_out, taps, filt, bias = pieces
    channels = query_feat.shape[0]
    rim = jnp.zeros((channels, SHORT - 1), jnp.bfloat16)
    query_conv, query_ext = short_forward(query_feat, rim, taps[0])
    key_conv, key_ext = short_forward(key_feat, rim, taps[1])
    value_conv, value_ext = short_forward(value_feat, rim, taps[2])
    product = (key_conv.astype(jnp.float32) * value_conv.astype(jnp.float32)).astype(jnp.bfloat16)
    filter_matrix = toeplitz(filt)
    blank = jnp.zeros((channels, TAPS), jnp.bfloat16)
    stacked_rows, grad_mixed, grad_qconv = mix_forward(query_conv, product, grad_out, filter_matrix, bias, blank)
    grad_product, filt_grad, bias_grad = mix_backward(stacked_rows, product, grad_mixed, filter_matrix, bias, blank)
    grad_kconv = (grad_product.astype(jnp.float32) * value_conv.astype(jnp.float32)).astype(jnp.bfloat16)
    grad_vconv = (grad_product.astype(jnp.float32) * key_conv.astype(jnp.float32)).astype(jnp.bfloat16)
    grad_query, tap_query = short_backward(grad_qconv, rim, taps[0], query_ext)
    grad_key, tap_key = short_backward(grad_kconv, rim, taps[1], key_ext)
    grad_value, tap_value = short_backward(grad_vconv, rim, taps[2], value_ext)
    return grad_query, grad_key, grad_value, jnp.stack([tap_query, tap_key, tap_value]), filt_grad, bias_grad


def reference(query_feat, key_feat, value_feat, grad_out, short_taps, filters, skip_bias):
    count = D // channel_block
    taps_blocks = short_taps.reshape(SHORT, SHORT, count, channel_block).transpose(2, 0, 1, 3)
    filt_blocks = filters.reshape(count, channel_block // GROUP, TAPS)
    bias_blocks = skip_bias.reshape(count, channel_block)
    results = lax.map(one_block, (query_feat.reshape(count, channel_block, LEN),
                                  key_feat.reshape(count, channel_block, LEN),
                                  value_feat.reshape(count, channel_block, LEN),
                                  grad_out.reshape(count, channel_block, LEN),
                                  taps_blocks, filt_blocks, bias_blocks))
    grad_query = results[0].reshape(D, LEN)
    grad_key = results[1].reshape(D, LEN)
    grad_value = results[2].reshape(D, LEN)
    grad_short = results[3].transpose(1, 2, 0, 3).reshape(SHORT, SHORT, D)
    grad_filters = results[4].reshape(D // GROUP, TAPS)
    grad_bias = results[5].reshape(D)
    return grad_query, grad_key, grad_value, grad_short, grad_filters, grad_bias
```

```python
import functools

import jax
import jax.numpy as jnp
from jax import lax
from jax.experimental import pallas as pl
from jax.experimental.pallas import tpu as pltpu
from jax.sharding import PartitionSpec as P

TAPS = 128
SHORT = 3
GROUP = 16
LANE = 128
TILE = 128
CHUNKS = 4
BF = jnp.bfloat16
F32 = jnp.float32
MESH = pl.DeviceIdType.MESH


def nn(a, b):
    return lax.dot_general(a, b, (((1,), (0,)), ((), ())), preferred_element_type=F32)


def nt(a, b):
    return lax.dot_general(a, b, (((1,), (1,)), ((), ())), preferred_element_type=F32)


def tn(a, b):
    return lax.dot_general(a, b, (((0,), (0,)), ((), ())), preferred_element_type=F32)


def iota(shape, axis):
    return lax.broadcasted_iota(jnp.int32, shape, axis)


def kernel(
    n, blocks,
    q_hbm, k_hbm, v_hbm, g_hbm, taps, fmsg,
    out_q, out_k, out_v, out_short, out_filt, out_bias,
    qx, kx, vx, gx, kc, vc, pr, gm, gw, acc, ph, gh, taps_b, bias_b,
    rim_s, rim_r, filt_s, filt_r, msg_s, msg_r, tot_s, tot_r, edge_s, edge_r,
    in_sem, rim_sem, ph_ssem, ph_rsem, gh_ssem, gh_rsem, filt_sem, msg_sem, tot_sem, edge_sem,
):
    me = lax.axis_index("ctx")
    channels = qx.shape[0]
    tiles = channels // TILE
    last = blocks - 1
    width = blocks * LANE
    chunks = min(CHUNKS, tiles)
    part = channels // chunks
    right, left = lax.rem(me + 1, n), lax.rem(me + n - 1, n)
    has_left, has_right = me > 0, me < n - 1
    tail = (blocks - 2) * LANE

    def piece(i, src, dst, start, size):
        cols = pl.ds(start, size)
        return pltpu.make_async_copy(src.at[:, cols], dst.at[:, cols], in_sem.at[i])

    loads = [
        piece(0, k_hbm, kx, tail, 2 * LANE),
        piece(1, v_hbm, vx, tail, 2 * LANE),
        piece(2, q_hbm, qx, tail, 2 * LANE),
        piece(3, k_hbm, kx, 0, tail),
        piece(4, v_hbm, vx, 0, tail),
        piece(5, q_hbm, qx, 0, tail),
        piece(6, g_hbm, gx, 0, width),
    ]
    for load in loads:
        load.start()

    barrier = pltpu.get_barrier_semaphore()

    def greet(d, carry):
        pl.semaphore_signal(
            barrier, inc=1, device_id={"ctx": lax.rem(me + d, n)}, device_id_type=MESH
        )
        return carry

    lax.fori_loop(1, n, greet, 0)

    lane16 = iota((GROUP, LANE), 1)
    first1, first2 = lane16 < 1, lane16 < 2
    last1, last2 = lane16 >= LANE - 1, lane16 >= LANE - 2
    zero16 = jnp.zeros((GROUP, LANE), BF)
    eye = iota((TILE, TILE), 0) == iota((TILE, TILE), 1)
    ones = jnp.ones((TILE, LANE), BF)

    def spread(row):
        return nn(jnp.where(eye, row, 0.0).astype(BF), ones).astype(BF)

    def tap_tile(t, carry):
        cols = pl.ds(pl.multiple_of(t * TILE, TILE), TILE)
        for w in range(3):
            for j in range(SHORT):
                taps_b[w * 3 + j, cols, :] = spread(taps[w, j : j + 1, cols])
        return carry

    lax.fori_loop(0, tiles, tap_tile, 0)

    own = fmsg[...]
    own_bias = pltpu.roll(own[2:3, :], lax.rem(me, 4) * 32, 1)
    filt_s[...] = jnp.concatenate([own[0:2], own_bias, jnp.zeros((5, LANE), F32)], axis=0)
    filt_r[me] = filt_s[...]

    sub8, lane8 = iota((8, LANE), 0), iota((8, LANE), 1)

    def pick(w, first_lane):
        return ((sub8 // 2 == w) & (lane8 == first_lane + sub8 % 2)).astype(F32).astype(BF)

    loads[0].wait()
    loads[1].wait()
    loads[2].wait()
    final = pl.ds(last * LANE, LANE)
    rim_s[...] = (
        nt(pick(0, LANE - 2), qx[:, final])
        + nt(pick(1, LANE - 2), kx[:, final])
        + nt(pick(2, LANE - 2), vx[:, final])
    )

    def shift_right(cur, prev, by, mask):
        before = zero16 if prev is None else pltpu.roll(prev, by, 1)
        return jnp.where(mask, before, pltpu.roll(cur, by, 1))

    def short_forward(w, rows, cur, prev):
        return (
            taps_b[w * 3, rows, :] * cur
            + taps_b[w * 3 + 1, rows, :] * shift_right(cur, prev, 1, first1)
            + taps_b[w * 3 + 2, rows, :] * shift_right(cur, prev, 2, first2)
        )

    def lanes(i):
        return pl.ds(i * LANE, LANE)

    def tail_rows(t, carry):
        for u in range(4):
            rows = pl.ds(pl.multiple_of(t * 64 + u * GROUP, GROUP), GROUP)
            kv = []
            for w, (src, dst) in ((1, (kx, kc)), (2, (vx, vc))):
                y = short_forward(w, rows, src[rows, lanes(last)], src[rows, lanes(last - 1)])
                dst[rows, lanes(last)] = y
                kv.append(y)
            pr[rows, lanes(last)] = kv[0] * kv[1]
        return carry

    lax.fori_loop(0, channels // 64, tail_rows, 0)

    pl.semaphore_wait(barrier, n - 1)

    rim_copy = pltpu.make_async_remote_copy(
        src_ref=rim_s, dst_ref=rim_r, send_sem=rim_sem.at[0], recv_sem=rim_sem.at[1],
        device_id={"ctx": right}, device_id_type=MESH,
    )

    def ph_copy(c):
        rows = pl.ds(c * part, part)
        return pltpu.make_async_remote_copy(
            src_ref=pr.at[rows, lanes(last)], dst_ref=ph.at[rows, :],
            send_sem=ph_ssem.at[c], recv_sem=ph_rsem.at[c],
            device_id={"ctx": right}, device_id_type=MESH,
        )

    def gh_copy(c):
        rows = pl.ds(c * part, part)
        return pltpu.make_async_remote_copy(
            src_ref=gm.at[rows, lanes(0)], dst_ref=gh.at[rows, :],
            send_sem=gh_ssem.at[c], recv_sem=gh_rsem.at[c],
            device_id={"ctx": left}, device_id_type=MESH,
        )

    @pl.when(has_right)
    def _():
        rim_copy.start()
        ph_copy(0).start()

    def filt_copy(d):
        return pltpu.make_async_remote_copy(
            src_ref=filt_s, dst_ref=filt_r.at[me], send_sem=filt_sem.at[0], recv_sem=filt_sem.at[1],
            device_id={"ctx": lax.rem(me + d, n)}, device_id_type=MESH,
        )

    def send_filt(d, carry):
        filt_copy(d).start()
        return carry

    lax.fori_loop(1, n, send_filt, 0)

    @pl.when(has_right)
    def _():
        for c in range(1, chunks):
            ph_copy(c).start()

    for load in loads[3:]:
        load.wait()

    def forward_rows(t, carry):
        for u in range(4):
            rows = pl.ds(pl.multiple_of(t * 64 + u * GROUP, GROUP), GROUP)
            for i in range(blocks):
                before = lambda src: None if i == 0 else src[rows, lanes(i - 1)]
                if i < last:
                    kk = short_forward(1, rows, kx[rows, lanes(i)], before(kx))
                    vv = short_forward(2, rows, vx[rows, lanes(i)], before(vx))
                    kc[rows, lanes(i)] = kk
                    vc[rows, lanes(i)] = vv
                    pr[rows, lanes(i)] = kk * vv
                qq = short_forward(0, rows, qx[rows, lanes(i)], before(qx))
                gm[rows, lanes(i)] = gx[rows, lanes(i)] * qq
        return carry

    lax.fori_loop(0, channels // 64, forward_rows, 0)

    @pl.when(has_left)
    def _():
        rim_copy.wait_recv()

    @pl.when(jnp.logical_not(has_left))
    def _():
        rim_r[...] = jnp.zeros(rim_r.shape, F32)
        ph[...] = jnp.zeros(ph.shape, BF)

    @pl.when(jnp.logical_not(has_right))
    def _():
        edge_r[...] = jnp.zeros(edge_r.shape, F32)
        gh[...] = jnp.zeros(gh.shape, BF)

    sub16, wide = iota((16, 3 * LANE), 0), iota((16, 3 * LANE), 1)

    def place(first_lane):
        hit = (sub16 // 2 == wide // LANE) & (wide % LANE == first_lane + sub16 % 2)
        return (hit & (sub16 < 6)).astype(F32).astype(BF)

    def head_tile(t, carry):
        cols = pl.ds(pl.multiple_of(t * TILE, TILE), TILE)
        x = rim_r[:, cols]
        rows = []
        for w in range(3):
            tap1, tap2 = taps[w, 1:2, cols], taps[w, 2:3, cols]
            x2, x1 = x[2 * w : 2 * w + 1], x[2 * w + 1 : 2 * w + 2]
            rows += [tap1 * x1 + tap2 * x2, tap2 * x1]
        rows.append(jnp.zeros((10, TILE), F32))
        fix = tn(jnp.concatenate(rows, axis=0).astype(BF), place(0)).astype(BF)
        kk = kc[cols, lanes(0)] + fix[:, LANE : 2 * LANE]
        vv = vc[cols, lanes(0)] + fix[:, 2 * LANE :]
        kc[cols, lanes(0)] = kk
        vc[cols, lanes(0)] = vv
        pr[cols, lanes(0)] = kk * vv
        gm[cols, lanes(0)] = gm[cols, lanes(0)] + gx[cols, lanes(0)] * fix[:, :LANE]
        return carry

    lax.fori_loop(0, tiles, head_tile, 0)

    @pl.when(has_left)
    def _():
        for c in range(chunks):
            gh_copy(c).start()

    def drain(ref, sem):
        pltpu.make_async_copy(ref, ref, sem).wait()

    others = pl.ds(0, n - 1)
    drain(filt_r.at[others], filt_sem.at[1])

    def bias_tile(t, carry):
        row = (
            filt_r[t * 4, 2:3, :] + filt_r[t * 4 + 1, 2:3, :]
            + filt_r[t * 4 + 2, 2:3, :] + filt_r[t * 4 + 3, 2:3, :]
        )
        bias_b[pl.ds(pl.multiple_of(t * TILE, TILE), TILE), :] = spread(row)
        return carry

    lax.fori_loop(0, tiles, bias_tile, 0)

    sq_row, sq_col = iota((LANE, LANE), 0), iota((LANE, LANE), 1)
    upper = sq_col >= sq_row
    late = sq_col + sq_row >= LANE - 1
    flip = (sq_col + sq_row == LANE - 1).astype(F32).astype(BF)
    zero_sq = jnp.zeros((LANE, LANE), BF)
    ones8 = jnp.ones((8, LANE), BF)

    def shift_left(cur, nxt, by, mask):
        after = zero16 if nxt is None else pltpu.roll(nxt, LANE - by, 1)
        return jnp.where(mask, after, pltpu.roll(cur, LANE - by, 1))

    def msg_copy(o):
        return pltpu.make_async_remote_copy(
            src_ref=msg_s.at[o], dst_ref=msg_r.at[me], send_sem=msg_sem.at[0], recv_sem=msg_sem.at[1],
            device_id={"ctx": o}, device_id_type=MESH,
        )

    def main_tile(t, carry):
        base = t * TILE

        for c in range(chunks):
            @pl.when(base == c * part)
            def _():
                @pl.when(has_left)
                def _():
                    ph_copy(c).wait_recv()

                @pl.when(has_right)
                def _():
                    gh_copy(c).wait_recv()

        for u in range(TILE // GROUP):
            rows = pl.ds(pl.multiple_of(base + u * GROUP, GROUP), GROUP)
            own_rows = pl.ds(u * GROUP, GROUP)
            slot = t * 4 + u // 2
            filt = filt_r[slot, u % 2 : u % 2 + 1, :].astype(BF)
            round_filt = pltpu.roll(
                jnp.broadcast_to(filt, (LANE, LANE)), 0, 1, stride=1, stride_axis=0
            )
            now = jnp.where(upper, round_filt, zero_sq)
            then = jnp.where(upper, zero_sq, round_filt)
            p = [pr[rows, lanes(i)] for i in range(blocks)]
            m = [gm[rows, lanes(i)] for i in range(blocks)]
            p_ext = jnp.concatenate([ph[rows, :]] + p, axis=0)
            m_all = jnp.concatenate(m, axis=0)
            m_next = jnp.concatenate(m[1:] + [gh[rows, :]], axis=0)
            depth = blocks * GROUP
            mixed = nn(
                jnp.concatenate([p_ext[:depth], p_ext[GROUP:]], axis=1),
                jnp.concatenate([then, now], axis=0),
            ).astype(BF)
            back = nt(
                jnp.concatenate([m_all, m_next], axis=1),
                jnp.concatenate([now, then], axis=1),
            ).astype(BF)
            p_turned = nt(flip, p_ext).astype(BF)
            pad = jnp.zeros((GROUP, LANE), BF)
            m_pair = jnp.concatenate(
                [jnp.concatenate([m_all, pad], axis=0), jnp.concatenate([pad, m_all], axis=0)], axis=1
            )
            diff = nn(p_turned, m_pair)
            diff = jnp.where(late, diff[:, LANE:], diff[:, :LANE])
            diff = pltpu.roll(diff, 1, 1, stride=1, stride_axis=0)
            msg_s[slot, u % 2 : u % 2 + 1, :] = jnp.sum(diff, axis=0, keepdims=True)

            bias = bias_b[rows, :]
            bias_sum = None
            for i in range(blocks):
                block = pl.ds(i * GROUP, GROUP)
                mixed_i = mixed[i * GROUP : (i + 1) * GROUP] + bias * p[i]
                back_i = back[i * GROUP : (i + 1) * GROUP] + bias * m[i]
                gw[0, own_rows, lanes(i)] = gx[rows, lanes(i)] * mixed_i
                gw[1, own_rows, lanes(i)] = back_i * vc[rows, lanes(i)]
                gw[2, own_rows, lanes(i)] = back_i * kc[rows, lanes(i)]
                term = m[i] * p[i]
                bias_sum = term if bias_sum is None else bias_sum + term
            acc[9, own_rows, :] = bias_sum

            for w, (src, dst) in enumerate(((qx, out_q), (kx, out_k), (vx, out_v))):
                sums = [None] * SHORT
                tap = [taps_b[w * 3 + j, rows, :] for j in range(SHORT)]
                for i in range(blocks):
                    g0 = gw[w, own_rows, lanes(i)]
                    nxt = None if i == last else gw[w, own_rows, lanes(i + 1)]
                    shifted = [g0, shift_left(g0, nxt, 1, last1), shift_left(g0, nxt, 2, last2)]
                    dst[rows, lanes(i)] = tap[0] * shifted[0] + tap[1] * shifted[1] + tap[2] * shifted[2]
                    x = src[rows, lanes(i)]
                    for j in range(SHORT):
                        term = shifted[j] * x
                        sums[j] = term if sums[j] is None else sums[j] + term
                for j in range(SHORT):
                    acc[w * 3 + j, own_rows, :] = sums[j]

        cols = pl.ds(pl.multiple_of(base, TILE), TILE)
        edge = (
            nt(pick(0, 0), gw[0, :, 0:LANE])
            + nt(pick(1, 0), gw[1, :, 0:LANE])
            + nt(pick(2, 0), gw[2, :, 0:LANE])
        )
        edge_s[:, cols] = edge
        x = rim_r[:, cols]
        bias_row = nt(ones8, acc[9])[0:1]
        for w in range(3):
            g0, g1 = edge[2 * w : 2 * w + 1], edge[2 * w + 1 : 2 * w + 2]
            x2, x1 = x[2 * w : 2 * w + 1], x[2 * w + 1 : 2 * w + 2]
            row0 = nt(ones8, acc[w * 3])[0:1]
            row1 = nt(ones8, acc[w * 3 + 1])[0:1] + g0 * x1
            row2 = nt(ones8, acc[w * 3 + 2])[0:1] + g0 * x2 + g1 * x1
            msg_s[t * 4 + w, 2:6, :] = jnp.concatenate([bias_row, row0, row1, row2], axis=0)
        msg_s[t * 4 + 3, 2:6, :] = jnp.concatenate(
            [bias_row, jnp.zeros((3, LANE), F32)], axis=0
        )
        for i in range(4):
            o = t * 4 + i

            @pl.when(o != me)
            def _():
                msg_copy(o).start()

        return carry

    def clear(o, carry):
        msg_s[o] = jnp.zeros((8, LANE), F32)
        return carry

    lax.fori_loop(0, n, clear, 0)
    lax.fori_loop(0, tiles, main_tile, 0)

    edge_copy = pltpu.make_async_remote_copy(
        src_ref=edge_s, dst_ref=edge_r, send_sem=edge_sem.at[0], recv_sem=edge_sem.at[1],
        device_id={"ctx": left}, device_id_type=MESH,
    )

    @pl.when(has_left)
    def _():
        edge_copy.start()

    msg_r[me] = msg_s[me]
    drain(msg_r.at[others], msg_sem.at[1])

    def add_up(o, total):
        return total + msg_r[o]

    total = lax.fori_loop(0, n, add_up, jnp.zeros((8, LANE), F32), unroll=8)
    out_filt[...] = total[0:2]
    out_bias[...] = pltpu.roll(total[2:3], lax.rem(LANE - lax.rem(me, 4) * 32, LANE), 1)
    tot_s[...] = jnp.concatenate([total[3:6], jnp.zeros((5, LANE), F32)], axis=0)
    tot_r[me] = tot_s[...]

    def tot_copy(d):
        return pltpu.make_async_remote_copy(
            src_ref=tot_s, dst_ref=tot_r.at[me], send_sem=tot_sem.at[0], recv_sem=tot_sem.at[1],
            device_id={"ctx": lax.rem(me + d, n)}, device_id_type=MESH,
        )

    def send_tot(d, carry):
        tot_copy(d).start()
        return carry

    lax.fori_loop(1, n, send_tot, 0)

    @pl.when(has_right)
    def _():
        edge_copy.wait_recv()

    def end_tile(t, carry):
        cols = pl.ds(pl.multiple_of(t * TILE, TILE), TILE)
        x = edge_r[:, cols]
        rows = []
        for w in range(3):
            tap1, tap2 = taps[w, 1:2, cols], taps[w, 2:3, cols]
            g0, g1 = x[2 * w : 2 * w + 1], x[2 * w + 1 : 2 * w + 2]
            rows += [tap2 * g0, tap1 * g0 + tap2 * g1]
        rows.append(jnp.zeros((10, TILE), F32))
        fix = tn(jnp.concatenate(rows, axis=0).astype(BF), place(LANE - 2)).astype(BF)
        for w, dst in enumerate((out_q, out_k, out_v)):
            dst[cols, lanes(last)] = dst[cols, lanes(last)] + fix[:, w * LANE : (w + 1) * LANE]
        return carry

    lax.fori_loop(0, tiles, end_tile, 0)

    drain(tot_r.at[others], tot_sem.at[1])
    for w in range(3):
        for t in range(tiles):
            out_short[w, :, t * TILE : (t + 1) * TILE] = tot_r[t * 4 + w, 0:SHORT, :]

    drain(filt_r.at[others], filt_sem.at[0])
    drain(msg_r.at[others], msg_sem.at[0])
    drain(tot_r.at[others], tot_sem.at[0])

    @pl.when(has_right)
    def _():
        rim_copy.wait_send()
        for c in range(chunks):
            ph_copy(c).wait_send()

    @pl.when(has_left)
    def _():
        edge_copy.wait_send()
        for c in range(chunks):
            gh_copy(c).wait_send()


def body(query_feat, key_feat, value_feat, grad_out, short_taps, filters, skip_bias):
    channels, length = query_feat.shape
    n = lax.axis_size("ctx")
    blocks = length // LANE
    bias_row = jnp.pad(skip_bias.astype(F32), (0, LANE - skip_bias.shape[0]))[None, :]
    fmsg = jnp.concatenate([filters.astype(F32), bias_row, jnp.zeros((5, LANE), F32)], axis=0)
    full = (channels, length)
    vmem = pl.BlockSpec(memory_space=pltpu.VMEM)
    hbm = pl.BlockSpec(memory_space=pl.ANY)
    outs = pl.pallas_call(
        functools.partial(kernel, n, blocks),
        out_shape=(
            pltpu.VMEM(full, BF), pltpu.VMEM(full, BF), pltpu.VMEM(full, BF),
            jax.ShapeDtypeStruct((3, SHORT, channels), F32),
            jax.ShapeDtypeStruct((2, LANE), F32),
            jax.ShapeDtypeStruct((1, LANE), F32),
        ),
        in_specs=[hbm] * 4 + [vmem] * 2,
        out_specs=(vmem,) * 6,
        scratch_shapes=[
            pltpu.VMEM(full, BF), pltpu.VMEM(full, BF), pltpu.VMEM(full, BF), pltpu.VMEM(full, BF),
            pltpu.VMEM(full, BF), pltpu.VMEM(full, BF), pltpu.VMEM(full, BF), pltpu.VMEM(full, BF),
            pltpu.VMEM((3, TILE, length), BF),
            pltpu.VMEM((10, TILE, LANE), BF),
            pltpu.VMEM((channels, LANE), BF), pltpu.VMEM((channels, LANE), BF),
            pltpu.VMEM((9, channels, LANE), BF),
            pltpu.VMEM((channels, LANE), BF),
            pltpu.VMEM((8, channels), F32), pltpu.VMEM((8, channels), F32),
            pltpu.VMEM((8, LANE), F32), pltpu.VMEM((n, 8, LANE), F32),
            pltpu.VMEM((n, 8, LANE), F32), pltpu.VMEM((n, 8, LANE), F32),
            pltpu.VMEM((8, LANE), F32), pltpu.VMEM((n, 8, LANE), F32),
            pltpu.VMEM((8, channels), F32), pltpu.VMEM((8, channels), F32),
            pltpu.SemaphoreType.DMA((7,)),
            pltpu.SemaphoreType.DMA((2,)),
            pltpu.SemaphoreType.DMA((CHUNKS,)), pltpu.SemaphoreType.DMA((CHUNKS,)),
            pltpu.SemaphoreType.DMA((CHUNKS,)), pltpu.SemaphoreType.DMA((CHUNKS,)),
            pltpu.SemaphoreType.DMA((2,)),
            pltpu.SemaphoreType.DMA((2,)),
            pltpu.SemaphoreType.DMA((2,)),
            pltpu.SemaphoreType.DMA((2,)),
        ],
        compiler_params=pltpu.CompilerParams(
            collective_id=0, has_side_effects=True, vmem_limit_bytes=48 * 1024 * 1024
        ),
    )(query_feat, key_feat, value_feat, grad_out, short_taps, fmsg)
    grad_query, grad_key, grad_value, grad_short, grad_filters, bias_out = outs
    return (
        grad_query, grad_key, grad_value, grad_short, grad_filters,
        bias_out[0, : skip_bias.shape[0]],
    )


def solution(mesh):
    in_specs = (
        P("tp", "ctx"),
        P("tp", "ctx"),
        P("tp", "ctx"),
        P("tp", "ctx"),
        P(None, None, "tp"),
        P(("tp", "ctx"), None),
        P(("tp", "ctx")),
    )
    out_specs = (
        P("tp", "ctx"),
        P("tp", "ctx"),
        P("tp", "ctx"),
        P(None, None, "tp"),
        P(("tp", "ctx"), None),
        P(("tp", "ctx")),
    )
    return jax.shard_map(body, mesh=mesh, in_specs=in_specs, out_specs=out_specs, check_vma=False)
```

```python
import functools

import jax
import jax.numpy as jnp
from jax import lax
from jax.experimental import pallas as pl
from jax.experimental.pallas import tpu as pltpu
from jax.sharding import PartitionSpec as P

TAPS = 128
SHORT = 3
GROUP = 16
LANE = 128
TILE = 128
CHUNKS = 4
BF = jnp.bfloat16
F32 = jnp.float32
MESH = pl.DeviceIdType.MESH


def nn(a, b):
    return lax.dot_general(a, b, (((1,), (0,)), ((), ())), preferred_element_type=F32)


def nt(a, b):
    return lax.dot_general(a, b, (((1,), (1,)), ((), ())), preferred_element_type=F32)


def tn(a, b):
    return lax.dot_general(a, b, (((0,), (0,)), ((), ())), preferred_element_type=F32)


def iota(shape, axis):
    return lax.broadcasted_iota(jnp.int32, shape, axis)


def lanes(i):
    return pl.ds(i * LANE, LANE)


def place(firsts):
    sub, lane = iota((16, LANE), 0), iota((16, LANE), 1)
    blocks = [
        ((sub // 2 == w) & (lane == first + sub % 2)).astype(F32).astype(BF)
        for w, first in enumerate(firsts)
    ]
    return jnp.concatenate(blocks, axis=1)


def kernel(
    n, blocks,
    q_hbm, k_hbm, v_hbm, g_hbm, taps_hbm, filt_hbm, bias_hbm,
    out_q, out_k, out_v, out_edge, out_short, out_filt, out_bias,
    qx, kx, vx, gx, kc, vc, pr, gm, gmr, conv, acc, heads, first, after, ph, gh, taps, filt_in, bias_in, taps_b, bias_b,
    rim_s, rim_r, col_s, col_r, filt_s, filt_r, msg_s, msg_r, tot_s, tot_r, edge_s, edge_r,
    in_sem, rim_sem, col_sem, ph_ssem, ph_rsem, gh_ssem, gh_rsem, filt_sem, msg_sem, tot_sem, edge_sem,
):
    me = lax.axis_index("ctx")
    channels = qx.shape[0]
    tiles = channels // TILE
    chunks = min(CHUNKS, tiles)
    last = blocks - 1
    part = channels // chunks
    right, left = lax.rem(me + 1, n), lax.rem(me + n - 1, n)
    has_left, has_right = me > 0, me < n - 1

    def piece(i, src, dst, start, size):
        cols = pl.ds(start * LANE, size * LANE)
        return pltpu.make_async_copy(src.at[:, cols], dst.at[:, cols], in_sem.at[i])

    loads = [
        pltpu.make_async_copy(taps_hbm, taps, in_sem.at[0]),
        pltpu.make_async_copy(filt_hbm, filt_in, in_sem.at[1]),
        pltpu.make_async_copy(bias_hbm, bias_in, in_sem.at[2]),
        piece(3, k_hbm, kx, blocks - 2, 2),
        piece(4, v_hbm, vx, blocks - 2, 2),
        piece(5, q_hbm, qx, last, 1),
        piece(6, q_hbm, qx, 0, 1),
        piece(7, g_hbm, gx, 0, 1),
        piece(8, k_hbm, kx, 0, blocks - 2),
        piece(9, v_hbm, vx, 0, blocks - 2),
        piece(10, q_hbm, qx, 1, blocks - 2),
        piece(11, g_hbm, gx, 1, blocks - 1),
    ]
    for load in loads:
        load.start()

    barrier = pltpu.get_barrier_semaphore()

    def greet(d, carry):
        pl.semaphore_signal(
            barrier, inc=1, device_id={"ctx": lax.rem(me + d, n)}, device_id_type=MESH
        )
        return carry

    lax.fori_loop(1, n, greet, 0)

    lane16 = iota((GROUP, LANE), 1)
    first1, first2 = lane16 < 1, lane16 < 2
    last1, last2 = lane16 >= LANE - 1, lane16 >= LANE - 2
    zero16 = jnp.zeros((GROUP, LANE), BF)
    eye = iota((TILE, TILE), 0) == iota((TILE, TILE), 1)
    ones = jnp.ones((TILE, LANE), BF)
    flip = (iota((LANE, LANE), 0) + iota((LANE, LANE), 1) == LANE - 1).astype(F32).astype(BF)

    def spread(row):
        return nn(jnp.where(eye, row, 0.0).astype(BF), ones).astype(BF)

    loads[0].wait()

    def tap_tile(t, carry):
        cols = pl.ds(pl.multiple_of(t * TILE, TILE), TILE)
        for w in range(3):
            for j in range(SHORT):
                taps_b[w * 3 + j, cols, :] = spread(taps[w, j : j + 1, cols])
        return carry

    lax.fori_loop(0, tiles, tap_tile, 0)

    loads[1].wait()
    loads[2].wait()
    own_bias = bias_in[...].astype(F32).reshape(1, -1)
    own_bias = jnp.pad(own_bias, ((0, 0), (0, LANE - own_bias.shape[1])))
    own_bias = pltpu.roll(own_bias, lax.rem(me, 4) * 32, 1)
    filt_s[...] = jnp.concatenate(
        [filt_in[...].astype(F32), own_bias, jnp.zeros((5, LANE), F32)], axis=0
    )
    filt_r[me] = filt_s[...]

    sub8, lane8 = iota((8, LANE), 0), iota((8, LANE), 1)

    def pick(w, first_lane):
        return ((sub8 // 2 == w) & (lane8 == first_lane + sub8 % 2)).astype(F32).astype(BF)

    def shift_right(cur, before, mask):
        return jnp.where(mask, zero16 if before is None else before, cur)

    def short_forward(tap, x, r1, r2, b1, b2):
        return tap[0] * x + tap[1] * shift_right(r1, b1, first1) + tap[2] * shift_right(r2, b2, first2)

    for load in loads[3:8]:
        load.wait()
    rim_s[...] = (
        nt(pick(0, LANE - 2), qx[:, lanes(last)])
        + nt(pick(1, LANE - 2), kx[:, lanes(last)])
        + nt(pick(2, LANE - 2), vx[:, lanes(last)])
    )
    col_s[...] = nt(pick(0, 0), gx[:, lanes(0)])

    def tap_of(w, rows):
        return [taps_b[w * 3 + j, rows, :] for j in range(SHORT)]

    def border_rows(t, carry):
        for u in range(4):
            rows = pl.ds(pl.multiple_of(t * 64 + u * GROUP, GROUP), GROUP)
            kv = []
            for w, (src, dst) in ((1, (kx, kc)), (2, (vx, vc))):
                x, prev = src[rows, lanes(last)], src[rows, lanes(last - 1)]
                y = short_forward(
                    tap_of(w, rows), x, pltpu.roll(x, 1, 1), pltpu.roll(x, 2, 1),
                    pltpu.roll(prev, 1, 1), pltpu.roll(prev, 2, 1),
                )
                dst[rows, lanes(last)] = y
                kv.append(y)
            pr[rows, lanes(last)] = kv[0] * kv[1]
            x = qx[rows, lanes(0)]
            y = short_forward(tap_of(0, rows), x, pltpu.roll(x, 1, 1), pltpu.roll(x, 2, 1), None, None)
            gm[rows, lanes(0)] = gx[rows, lanes(0)] * y
        return carry

    lax.fori_loop(0, channels // 64, border_rows, 0)

    pl.semaphore_wait(barrier, n - 1)

    rim_copy = pltpu.make_async_remote_copy(
        src_ref=rim_s, dst_ref=rim_r, send_sem=rim_sem.at[0], recv_sem=rim_sem.at[1],
        device_id={"ctx": right}, device_id_type=MESH,
    )
    col_copy = pltpu.make_async_remote_copy(
        src_ref=col_s, dst_ref=col_r, send_sem=col_sem.at[0], recv_sem=col_sem.at[1],
        device_id={"ctx": left}, device_id_type=MESH,
    )

    def ph_copy(c):
        rows = pl.ds(c * part, part)
        return pltpu.make_async_remote_copy(
            src_ref=pr.at[rows, lanes(last)], dst_ref=ph.at[rows, :],
            send_sem=ph_ssem.at[c], recv_sem=ph_rsem.at[c],
            device_id={"ctx": right}, device_id_type=MESH,
        )

    def gh_copy(c):
        rows = pl.ds(c * part, part)
        return pltpu.make_async_remote_copy(
            src_ref=gm.at[rows, lanes(0)], dst_ref=gh.at[rows, :],
            send_sem=gh_ssem.at[c], recv_sem=gh_rsem.at[c],
            device_id={"ctx": left}, device_id_type=MESH,
        )

    @pl.when(has_right)
    def _():
        rim_copy.start()
        ph_copy(0).start()

    @pl.when(has_left)
    def _():
        col_copy.start()
        gh_copy(0).start()

    def filt_copy(d):
        return pltpu.make_async_remote_copy(
            src_ref=filt_s, dst_ref=filt_r.at[me], send_sem=filt_sem.at[0], recv_sem=filt_sem.at[1],
            device_id={"ctx": lax.rem(me + d, n)}, device_id_type=MESH,
        )

    def send_filt(d, carry):
        filt_copy(d).start()
        return carry

    lax.fori_loop(1, n, send_filt, 0)

    @pl.when(has_right)
    def _():
        for c in range(1, chunks):
            ph_copy(c).start()

    @pl.when(has_left)
    def _():
        for c in range(1, chunks):
            gh_copy(c).start()

    for load in loads[8:]:
        load.wait()

    def forward_rows(t, carry):
        turned = []
        for u in range(4):
            rows = pl.ds(pl.multiple_of(t * 64 + u * GROUP, GROUP), GROUP)
            taps3 = [tap_of(w, rows) for w in range(3)]
            b1, b2 = [None] * 3, [None] * 3
            for i in range(blocks):
                short = [None] * 3
                for w, src in enumerate((qx, kx, vx)):
                    if i == last and w > 0:
                        continue
                    x = src[rows, lanes(i)]
                    r1, r2 = pltpu.roll(x, 1, 1), pltpu.roll(x, 2, 1)
                    if i > 0 or w > 0:
                        short[w] = short_forward(taps3[w], x, r1, r2, b1[w], b2[w])
                    b1[w], b2[w] = r1, r2
                if i < last:
                    kc[rows, lanes(i)] = short[1]
                    vc[rows, lanes(i)] = short[2]
                    pr[rows, lanes(i)] = short[1] * short[2]
                if i > 0:
                    m = gx[rows, lanes(i)] * short[0]
                    gm[rows, lanes(i)] = m
                    turned.append(m)
        turned = nn(jnp.concatenate(turned, axis=0), flip).astype(BF)
        for u in range(4):
            rows = pl.ds(pl.multiple_of(t * 64 + u * GROUP, GROUP), GROUP)
            for i in range(1, blocks):
                at = (u * last + i - 1) * GROUP
                gmr[rows, lanes(i)] = turned[at : at + GROUP]
        return carry

    lax.fori_loop(0, channels // 64, forward_rows, 0)

    @pl.when(has_left)
    def _():
        rim_copy.wait_recv()

    @pl.when(jnp.logical_not(has_left))
    def _():
        rim_r[...] = jnp.zeros(rim_r.shape, F32)
        ph[...] = jnp.zeros(ph.shape, BF)

    @pl.when(has_right)
    def _():
        col_copy.wait_recv()

    @pl.when(jnp.logical_not(has_right))
    def _():
        col_r[...] = jnp.zeros(col_r.shape, F32)
        edge_r[...] = jnp.zeros(edge_r.shape, F32)
        gh[...] = jnp.zeros(gh.shape, BF)

    def drain(ref, sem):
        pltpu.make_async_copy(ref, ref, sem).wait()

    others = pl.ds(0, n - 1)
    drain(filt_r.at[others], filt_sem.at[1])

    sq_row, sq_col = iota((LANE, LANE), 0), iota((LANE, LANE), 1)
    upper = sq_col >= sq_row
    early = sq_col + sq_row <= LANE - 1
    zero_sq = jnp.zeros((LANE, LANE), BF)
    rim_place = place((0, 0, 0, 0))
    pad = jnp.zeros((GROUP, LANE), BF)

    def shift_left(cur, after, mask):
        return jnp.where(mask, zero16 if after is None else after, cur)

    def msg_copy(o):
        return pltpu.make_async_remote_copy(
            src_ref=msg_s.at[o], dst_ref=msg_r.at[me], send_sem=msg_sem.at[0], recv_sem=msg_sem.at[1],
            device_id={"ctx": o}, device_id_type=MESH,
        )

    def halo_ready(base):
        for c in range(chunks):
            @pl.when(base == c * part)
            def _():
                @pl.when(has_left)
                def _():
                    ph_copy(c).wait_recv()

                @pl.when(has_right)
                def _():
                    gh_copy(c).wait_recv()

    def rims_in(t):
        cols = pl.ds(pl.multiple_of(t * TILE, TILE), TILE)
        rim, own, far = rim_r[:, cols], rim_s[:, cols], col_r[:, cols]
        rows = []
        for w in range(3):
            tap1, tap2 = taps[w, 1:2, cols], taps[w, 2:3, cols]
            x2, x1 = rim[2 * w : 2 * w + 1], rim[2 * w + 1 : 2 * w + 2]
            rows += [tap1 * x1 + tap2 * x2, tap2 * x1]
        tap1, tap2 = taps[0, 1:2, cols], taps[0, 2:3, cols]
        rows += [far[0:1] * (tap1 * own[1:2] + tap2 * own[0:1]), far[1:2] * (tap2 * own[1:2])]
        rows.append(jnp.zeros((8, TILE), F32))
        fix = tn(jnp.concatenate(rows, axis=0).astype(BF), rim_place).astype(BF)
        kk = kc[cols, lanes(0)] + fix[:, LANE : 2 * LANE]
        vv = vc[cols, lanes(0)] + fix[:, 2 * LANE : 3 * LANE]
        kc[cols, lanes(0)] = kk
        vc[cols, lanes(0)] = vv
        pr[cols, lanes(0)] = kk * vv
        m0 = gm[cols, lanes(0)] + gx[cols, lanes(0)] * fix[:, :LANE]
        first[cols, :] = m0
        gmr[cols, lanes(0)] = nn(m0, flip).astype(BF)
        after[cols, :] = gh[cols, :] + fix[:, 3 * LANE :]
        bias_b[cols, :] = spread(
            filt_r[t * 4, 2:3, :] + filt_r[t * 4 + 1, 2:3, :]
            + filt_r[t * 4 + 2, 2:3, :] + filt_r[t * 4 + 3, 2:3, :]
        )

    depth = blocks * GROUP

    def matmuls(t, u):
        rows = pl.ds(pl.multiple_of(t * TILE + u * GROUP, GROUP), GROUP)
        slot = t * 4 + u // 2
        filt = filt_r[slot, u % 2 : u % 2 + 1, :].astype(BF)
        round_filt = pltpu.roll(jnp.broadcast_to(filt, (LANE, LANE)), 0, 1, stride=1, stride_axis=0)
        now = jnp.where(upper, round_filt, zero_sq)
        then = jnp.where(upper, zero_sq, round_filt)
        p = [ph[rows, :]] + [pr[rows, lanes(i)] for i in range(blocks)]
        m = [first[rows, :]] + [gm[rows, lanes(i)] for i in range(1, blocks)] + [after[rows, :]]
        p_ext = jnp.concatenate(p, axis=0)
        m_ext = jnp.concatenate(m, axis=0)
        conv[u % 2, 0] = nn(
            jnp.concatenate([p_ext[:depth], p_ext[GROUP:]], axis=1),
            jnp.concatenate([then, now], axis=0),
        ).astype(BF)
        conv[u % 2, 1] = nt(
            jnp.concatenate([m_ext[:depth], m_ext[GROUP:]], axis=1),
            jnp.concatenate([now, then], axis=1),
        ).astype(BF)
        m_rev = [gmr[rows, lanes(i)] for i in range(blocks)]
        diff = tn(
            p_ext,
            jnp.concatenate(
                [jnp.concatenate(m_rev + [pad], axis=0), jnp.concatenate([pad] + m_rev, axis=0)], axis=1
            ),
        )
        diff = jnp.where(early, diff[:, LANE:], diff[:, :LANE]).astype(BF)
        diff = pltpu.roll(diff, 0, 1, stride=1, stride_axis=0)
        msg_s[slot, u % 2 : u % 2 + 1, :] = jnp.sum(diff.astype(F32), axis=0, keepdims=True)

    def gradients(t, u):
        rows = pl.ds(pl.multiple_of(t * TILE + u * GROUP, GROUP), GROUP)
        own_rows = pl.ds(u * GROUP, GROUP)
        bias = bias_b[rows, :]
        bias_sum = None
        gw = [[None] * blocks for _ in range(3)]
        for i in range(blocks):
            p = pr[rows, lanes(i)]
            m = first[rows, :] if i == 0 else gm[rows, lanes(i)]
            mixed = conv[u % 2, 0, pl.ds(i * GROUP, GROUP), :] + bias * p
            back = conv[u % 2, 1, pl.ds(i * GROUP, GROUP), :] + bias * m
            gw[0][i] = gx[rows, lanes(i)] * mixed
            gw[1][i] = back * vc[rows, lanes(i)]
            gw[2][i] = back * kc[rows, lanes(i)]
            term = m * p
            bias_sum = term if bias_sum is None else bias_sum + term
        acc[lax.rem(t, 2), 9, own_rows, :] = bias_sum
        for w, (src, dst) in enumerate(((qx, out_q), (kx, out_k), (vx, out_v))):
            sums = [None] * SHORT
            tap = tap_of(w, rows)
            a1 = a2 = None
            for i in reversed(range(blocks)):
                g0 = gw[w][i]
                r1, r2 = pltpu.roll(g0, LANE - 1, 1), pltpu.roll(g0, LANE - 2, 1)
                shifted = [g0, shift_left(r1, a1, last1), shift_left(r2, a2, last2)]
                a1, a2 = r1, r2
                dst[rows, lanes(i)] = tap[0] * shifted[0] + tap[1] * shifted[1] + tap[2] * shifted[2]
                x = src[rows, lanes(i)]
                for j in range(SHORT):
                    term = shifted[j] * x
                    sums[j] = term if sums[j] is None else sums[j] + term
            for j in range(SHORT):
                acc[lax.rem(t, 2), w * 3 + j, own_rows, :] = sums[j]
            heads[lax.rem(t, 2), w, own_rows, :] = gw[w][0]

    halves = ((iota((8, 2 * LANE), 1) // LANE) == iota((8, 2 * LANE), 0)).astype(F32).astype(BF)

    def lane_sums(a, b, c, d):
        sums = nt(
            halves,
            jnp.concatenate(
                [jnp.concatenate([a, b], axis=1), jnp.concatenate([c, d], axis=1)], axis=0
            ),
        )
        return [sums[0:1, :LANE], sums[1:2, :LANE], sums[0:1, LANE:], sums[1:2, LANE:]]

    def tile_sums(t):
        cols = pl.ds(pl.multiple_of(t * TILE, TILE), TILE)
        k = lax.rem(t, 2)
        edge = (
            nt(pick(0, 0), heads[k, 0]) + nt(pick(1, 0), heads[k, 1]) + nt(pick(2, 0), heads[k, 2])
        )
        edge_s[:, cols] = edge
        rim = rim_r[:, cols]
        sums = lane_sums(acc[k, 0], acc[k, 1], acc[k, 2], acc[k, 3])
        sums += lane_sums(acc[k, 4], acc[k, 5], acc[k, 6], acc[k, 7])
        sums += lane_sums(acc[k, 8], acc[k, 9], acc[k, 8], acc[k, 9])
        blank = jnp.zeros((2, LANE), F32)
        for w in range(3):
            g0, g1 = edge[2 * w : 2 * w + 1], edge[2 * w + 1 : 2 * w + 2]
            x2, x1 = rim[2 * w : 2 * w + 1], rim[2 * w + 1 : 2 * w + 2]
            row1 = sums[w * 3 + 1] + g0 * x1
            row2 = sums[w * 3 + 2] + g0 * x2 + g1 * x1
            msg_s[t * 4 + w, 2:8, :] = jnp.concatenate([sums[9], sums[w * 3], row1, row2, blank], axis=0)
        msg_s[t * 4 + 3, 2:8, :] = jnp.concatenate([sums[9], blank, blank, blank[:1]], axis=0)

    def send_sums(t):
        for i in range(4):
            o = t * 4 + i

            @pl.when(o != me)
            def _():
                msg_copy(o).start()

    def main_tile(t, before, ahead):
        if ahead:
            halo_ready((t + 1) * TILE)
        steps = TILE // GROUP
        matmuls(t, 0)
        if before:
            tile_sums(t - 1)
        for u in range(steps):
            if u + 1 < steps:
                matmuls(t, u + 1)
            if ahead and u == 2:
                rims_in(t + 1)
            gradients(t, u)
        if before:
            send_sums(t - 1)

    def middle_tile(t, carry):
        main_tile(t, True, True)
        return carry

    halo_ready(0)
    rims_in(0)
    main_tile(0, False, True)
    lax.fori_loop(1, tiles - 1, middle_tile, 0)
    main_tile(tiles - 1, True, False)
    tile_sums(tiles - 1)
    send_sums(tiles - 1)

    edge_copy = pltpu.make_async_remote_copy(
        src_ref=edge_s, dst_ref=edge_r, send_sem=edge_sem.at[0], recv_sem=edge_sem.at[1],
        device_id={"ctx": left}, device_id_type=MESH,
    )

    @pl.when(has_left)
    def _():
        edge_copy.start()

    msg_r[me] = msg_s[me]
    drain(msg_r.at[others], msg_sem.at[1])

    total = msg_r[0]
    for o in range(1, n):
        total = total + msg_r[o]
    tot_s[...] = jnp.concatenate([total[3:6], jnp.zeros((5, LANE), F32)], axis=0)

    def tot_copy(d):
        return pltpu.make_async_remote_copy(
            src_ref=tot_s, dst_ref=tot_r.at[me], send_sem=tot_sem.at[0], recv_sem=tot_sem.at[1],
            device_id={"ctx": lax.rem(me + d, n)}, device_id_type=MESH,
        )

    def send_tot(d, carry):
        tot_copy(d).start()
        return carry

    lax.fori_loop(1, n, send_tot, 0)
    tot_r[me] = tot_s[...]
    out_filt[...] = lax.dot_general(
        total, flip.astype(F32), (((1,), (0,)), ((), ())),
        preferred_element_type=F32, precision=lax.Precision.HIGHEST,
    )[0:2]
    out_bias[...] = pltpu.roll(total[2:3], lax.rem(LANE - lax.rem(me, 4) * 32, LANE), 1)

    @pl.when(has_right)
    def _():
        edge_copy.wait_recv()

    out_edge[...] = edge_r[...]

    drain(filt_r.at[others], filt_sem.at[0])
    drain(msg_r.at[others], msg_sem.at[0])

    @pl.when(has_right)
    def _():
        rim_copy.wait_send()
        for c in range(chunks):
            ph_copy(c).wait_send()

    @pl.when(has_left)
    def _():
        col_copy.wait_send()
        edge_copy.wait_send()
        for c in range(chunks):
            gh_copy(c).wait_send()

    drain(tot_r.at[others], tot_sem.at[1])
    for w in range(3):
        for t in range(tiles):
            out_short[w, :, t * TILE : (t + 1) * TILE] = tot_r[t * 4 + w, 0:SHORT, :]
    drain(tot_r.at[others], tot_sem.at[0])


def finish(
    blocks,
    gq, gk, gv, edge, short, filt, bias, taps_hbm,
    out_q, out_k, out_v, out_short, out_filt, out_bias,
    taps, ends, bias_v, sem, end_sem,
):
    last = blocks - 1
    bulk = pl.ds(0, last * LANE)
    copies = [pltpu.make_async_copy(taps_hbm, taps, sem.at[0])]
    for i, (src, dst) in enumerate(((gq, out_q), (gk, out_k), (gv, out_v))):
        copies.append(pltpu.make_async_copy(src.at[:, bulk], dst.at[:, bulk], sem.at[1 + i]))
    copies.append(pltpu.make_async_copy(short, out_short, sem.at[4]))
    copies.append(pltpu.make_async_copy(filt, out_filt, sem.at[5]))
    for copy in copies:
        copy.start()
    bias_v[...] = bias[0, : bias_v.shape[0]]
    copies.append(pltpu.make_async_copy(bias_v, out_bias, sem.at[6]))
    copies[-1].start()
    copies[0].wait()
    rim_place = place((LANE - 2, LANE - 2, LANE - 2))
    for t in range(gq.shape[0] // TILE):
        cols = pl.ds(t * TILE, TILE)
        x = edge[:, cols]
        rows = []
        for w in range(3):
            tap1, tap2 = taps[w, 1:2, cols], taps[w, 2:3, cols]
            g0, g1 = x[2 * w : 2 * w + 1], x[2 * w + 1 : 2 * w + 2]
            rows += [tap2 * g0, tap1 * g0 + tap2 * g1]
        rows.append(jnp.zeros((10, TILE), F32))
        fix = tn(jnp.concatenate(rows, axis=0).astype(BF), rim_place).astype(BF)
        for w, src in enumerate((gq, gk, gv)):
            ends[w, cols, :] = src[cols, lanes(last)] + fix[:, w * LANE : (w + 1) * LANE]
    for w, dst in enumerate((out_q, out_k, out_v)):
        copies.append(pltpu.make_async_copy(ends.at[w], dst.at[:, lanes(last)], end_sem.at[w]))
        copies[-1].start()
    for copy in copies[1:]:
        copy.wait()


def body(query_feat, key_feat, value_feat, grad_out, short_taps, filters, skip_bias):
    channels, length = query_feat.shape
    n = lax.axis_size("ctx")
    blocks = length // LANE
    full, tile = (channels, length), (channels, LANE)
    vmem = pl.BlockSpec(memory_space=pltpu.VMEM)
    hbm = pl.BlockSpec(memory_space=pltpu.HBM)
    dma = pltpu.SemaphoreType.DMA
    row = pltpu.VMEM((8, channels), F32)
    slots = pltpu.VMEM((n, 8, LANE), F32)
    one = pltpu.VMEM((8, LANE), F32)
    outs = pl.pallas_call(
        functools.partial(kernel, n, blocks),
        out_shape=(
            pltpu.VMEM(full, BF), pltpu.VMEM(full, BF), pltpu.VMEM(full, BF),
            row,
            pltpu.VMEM(short_taps.shape, F32),
            pltpu.VMEM(filters.shape, F32),
            pltpu.VMEM((1, LANE), F32),
        ),
        in_specs=[hbm] * 7,
        out_specs=(vmem,) * 7,
        scratch_shapes=[pltpu.VMEM(full, BF)] * 9
        + [
            pltpu.VMEM((2, 2, blocks * GROUP, LANE), BF),
            pltpu.VMEM((2, 10, TILE, LANE), BF),
            pltpu.VMEM((2, 3, TILE, LANE), BF),
            pltpu.VMEM(tile, BF), pltpu.VMEM(tile, BF),
            pltpu.VMEM(tile, BF), pltpu.VMEM(tile, BF),
            pltpu.VMEM(short_taps.shape, F32),
            pltpu.VMEM(filters.shape, BF),
            pltpu.VMEM(skip_bias.shape, BF),
            pltpu.VMEM((9, channels, LANE), BF),
            pltpu.VMEM(tile, BF),
            row, row, row, row, one, slots, slots, slots, one, slots, row, row,
            dma((12,)), dma((2,)), dma((2,)),
            dma((CHUNKS,)), dma((CHUNKS,)), dma((CHUNKS,)), dma((CHUNKS,)),
            dma((2,)), dma((2,)), dma((2,)), dma((2,)),
        ],
        compiler_params=pltpu.CompilerParams(
            collective_id=0, has_side_effects=True, vmem_limit_bytes=48 * 1024 * 1024
        ),
    )(query_feat, key_feat, value_feat, grad_out, short_taps, filters, skip_bias)
    return pl.pallas_call(
        functools.partial(finish, blocks),
        out_shape=tuple(
            jax.ShapeDtypeStruct(s, d)
            for s, d in (
                (full, BF), (full, BF), (full, BF),
                (short_taps.shape, F32), (filters.shape, F32), (skip_bias.shape, F32),
            )
        ),
        in_specs=[vmem] * 7 + [hbm],
        out_specs=(hbm,) * 6,
        scratch_shapes=[
            pltpu.VMEM(short_taps.shape, F32),
            pltpu.VMEM((3,) + tile, BF),
            pltpu.VMEM(skip_bias.shape, F32),
            dma((7,)), dma((3,)),
        ],
        compiler_params=pltpu.CompilerParams(vmem_limit_bytes=16 * 1024 * 1024),
    )(*outs, short_taps)


def solution(mesh):
    wide, narrow = P("tp", "ctx"), P(None, None, "tp")
    both = ("tp", "ctx")

    def whole(*args):
        with jax.sharding.use_abstract_mesh(mesh.abstract_mesh):
            return jax.shard_map(
                body,
                mesh=mesh,
                in_specs=(wide, wide, wide, wide, narrow, P(both, None), P(both)),
                out_specs=(wide, wide, wide, narrow, P(both, None), P(both)),
                check_vma=False,
            )(*args)

    return whole
```

```python
import functools

import jax
import jax.numpy as jnp
from jax import lax
from jax.experimental import pallas as pl
from jax.experimental.pallas import tpu as pltpu
from jax.sharding import PartitionSpec as P

TAPS = 128
SHORT = 3
GROUP = 16
LANE = 128
TILE = 128
CHUNKS = 4
BF = jnp.bfloat16
F32 = jnp.float32
MESH = pl.DeviceIdType.MESH


def nn(a, b):
    return lax.dot_general(a, b, (((1,), (0,)), ((), ())), preferred_element_type=F32)


def nt(a, b):
    return lax.dot_general(a, b, (((1,), (1,)), ((), ())), preferred_element_type=F32)


def tn(a, b):
    return lax.dot_general(a, b, (((0,), (0,)), ((), ())), preferred_element_type=F32)


def iota(shape, axis):
    return lax.broadcasted_iota(jnp.int32, shape, axis)


def lanes(i):
    return pl.ds(i * LANE, LANE)


def place(firsts):
    sub, lane = iota((16, LANE), 0), iota((16, LANE), 1)
    blocks = [
        ((sub // 2 == w) & (lane == first + sub % 2)).astype(F32).astype(BF)
        for w, first in enumerate(firsts)
    ]
    return jnp.concatenate(blocks, axis=1)


def kernel(
    n, blocks,
    q_hbm, k_hbm, v_hbm, g_hbm, taps_hbm, filt_hbm, bias_hbm,
    out_q, out_k, out_v, out_edge, out_short, out_filt, out_bias,
    qx, kx, vx, gx, kc, vc, pr, gm, gmr, raw, xs, conv, acc, heads, first, after, ph, gh, taps, filt_in, bias_in, taps_b, bias_b,
    rim_s, rim_r, col_s, col_r, filt_s, filt_r, msg_s, msg_r, tot_s, tot_r, edge_s, edge_r,
    in_sem, rim_sem, col_sem, ph_ssem, ph_rsem, gh_ssem, gh_rsem, filt_sem, msg_sem, tot_sem, edge_sem,
):
    me = lax.axis_index("ctx")
    channels = qx.shape[0]
    tiles = channels // TILE
    chunks = min(CHUNKS, tiles)
    last = blocks - 1
    part = channels // chunks
    right, left = lax.rem(me + 1, n), lax.rem(me + n - 1, n)
    has_left, has_right = me > 0, me < n - 1

    def peer(k):
        if n != 32:
            return lax.rem(me + 1 + k, n)
        i, j = k // 8, k // 2 % 4
        dz = 1 + 2 * i - 3 * (i // 2)
        dx = 2 - j + 3 * (j // 2) + 2 * (j // 3)
        z, x, c = (me // 8 + dz) % 4, (me // 2 + dx) % 4, (me + 1 + k % 2) % 2
        return z * 8 + x * 2 + c

    def piece(i, src, dst, start, size):
        cols = pl.ds(start * LANE, size * LANE)
        return pltpu.make_async_copy(src.at[:, cols], dst.at[:, cols], in_sem.at[i])

    loads = [
        pltpu.make_async_copy(taps_hbm, taps, in_sem.at[0]),
        pltpu.make_async_copy(filt_hbm, filt_in, in_sem.at[1]),
        pltpu.make_async_copy(bias_hbm, bias_in, in_sem.at[2]),
        piece(3, k_hbm, kx, blocks - 2, 2),
        piece(4, v_hbm, vx, blocks - 2, 2),
        piece(5, q_hbm, qx, last, 1),
        piece(6, q_hbm, qx, 0, 1),
        piece(7, g_hbm, gx, 0, 1),
        piece(8, k_hbm, kx, 0, blocks - 2),
        piece(9, v_hbm, vx, 0, blocks - 2),
        piece(10, q_hbm, qx, 1, blocks - 2),
        piece(11, g_hbm, gx, 1, blocks - 1),
    ]
    for load in loads:
        load.start()

    barrier = pltpu.get_barrier_semaphore()

    def greet(d, carry):
        pl.semaphore_signal(
            barrier, inc=1, device_id={"ctx": lax.rem(me + d, n)}, device_id_type=MESH
        )
        return carry

    lax.fori_loop(1, n, greet, 0)

    lane16 = iota((GROUP, LANE), 1)
    first1, first2 = lane16 < 1, lane16 < 2
    last1, last2 = lane16 >= LANE - 1, lane16 >= LANE - 2
    zero16 = jnp.zeros((GROUP, LANE), BF)
    eye = iota((TILE, TILE), 0) == iota((TILE, TILE), 1)
    ones = jnp.ones((TILE, LANE), BF)
    flip = (iota((LANE, LANE), 0) + iota((LANE, LANE), 1) == LANE - 1).astype(F32).astype(BF)

    def spread(row):
        return nn(jnp.where(eye, row, 0.0).astype(BF), ones).astype(BF)

    def tap_tile(t):
        cols = pl.ds(pl.multiple_of(t * TILE, TILE), TILE)
        for w in range(3):
            for j in range(SHORT):
                taps_b[w * 3 + j, cols, :] = spread(taps[w, j : j + 1, cols])

    loads[0].wait()
    tap_tile(0)

    loads[1].wait()
    loads[2].wait()
    own_bias = bias_in[...].astype(F32).reshape(1, -1)
    own_bias = jnp.pad(own_bias, ((0, 0), (0, LANE - own_bias.shape[1])))
    own_bias = pltpu.roll(own_bias, lax.rem(me, 4) * 32, 1)
    filt_s[...] = jnp.concatenate(
        [filt_in[...].astype(F32), own_bias, jnp.zeros((5, LANE), F32)], axis=0
    )
    filt_r[me] = filt_s[...]

    sub8, lane8 = iota((8, LANE), 0), iota((8, LANE), 1)

    def pick(w, first_lane):
        return ((sub8 // 2 == w) & (lane8 == first_lane + sub8 % 2)).astype(F32).astype(BF)

    def shift_right(cur, before, mask):
        return jnp.where(mask, zero16 if before is None else before, cur)

    def short_forward(w, rows, i, tap, x, r1, r2, b1, b2):
        s1, s2 = shift_right(r1, b1, first1), shift_right(r2, b2, first2)
        xs[w, 0, rows, lanes(i)] = s1
        xs[w, 1, rows, lanes(i)] = s2
        return tap[0] * x + tap[1] * s1 + tap[2] * s2

    for load in loads[3:8]:
        load.wait()
    rim_s[...] = (
        nt(pick(0, LANE - 2), qx[:, lanes(last)])
        + nt(pick(1, LANE - 2), kx[:, lanes(last)])
        + nt(pick(2, LANE - 2), vx[:, lanes(last)])
    )
    col_s[...] = nt(pick(0, 0), gx[:, lanes(0)])

    def tap_of(w, rows):
        return [taps_b[w * 3 + j, rows, :] for j in range(SHORT)]

    def border_tile(t):
        for u in range(TILE // GROUP):
            rows = pl.ds(pl.multiple_of(t * TILE + u * GROUP, GROUP), GROUP)
            kv = []
            for w, (src, dst) in ((1, (kx, kc)), (2, (vx, vc))):
                x, prev = src[rows, lanes(last)], src[rows, lanes(last - 1)]
                y = short_forward(
                    w, rows, last, tap_of(w, rows), x, pltpu.roll(x, 1, 1), pltpu.roll(x, 2, 1),
                    pltpu.roll(prev, 1, 1), pltpu.roll(prev, 2, 1),
                )
                dst[rows, lanes(last)] = y
                kv.append(y)
            pr[rows, lanes(last)] = kv[0] * kv[1]
            x = qx[rows, lanes(0)]
            y = short_forward(
                0, rows, 0, tap_of(0, rows), x, pltpu.roll(x, 1, 1), pltpu.roll(x, 2, 1), None, None
            )
            gm[rows, lanes(0)] = gx[rows, lanes(0)] * y

    def start_tile(t, carry):
        tap_tile(t)
        border_tile(t - 1)
        return carry

    lax.fori_loop(1, tiles, start_tile, 0)
    border_tile(tiles - 1)

    pl.semaphore_wait(barrier, n - 1)

    rim_copy = pltpu.make_async_remote_copy(
        src_ref=rim_s, dst_ref=rim_r, send_sem=rim_sem.at[0], recv_sem=rim_sem.at[1],
        device_id={"ctx": right}, device_id_type=MESH,
    )
    col_copy = pltpu.make_async_remote_copy(
        src_ref=col_s, dst_ref=col_r, send_sem=col_sem.at[0], recv_sem=col_sem.at[1],
        device_id={"ctx": left}, device_id_type=MESH,
    )

    def ph_copy(c):
        rows = pl.ds(c * part, part)
        return pltpu.make_async_remote_copy(
            src_ref=pr.at[rows, lanes(last)], dst_ref=ph.at[rows, :],
            send_sem=ph_ssem.at[c], recv_sem=ph_rsem.at[c],
            device_id={"ctx": right}, device_id_type=MESH,
        )

    def gh_copy(c):
        rows = pl.ds(c * part, part)
        return pltpu.make_async_remote_copy(
            src_ref=gm.at[rows, lanes(0)], dst_ref=gh.at[rows, :],
            send_sem=gh_ssem.at[c], recv_sem=gh_rsem.at[c],
            device_id={"ctx": left}, device_id_type=MESH,
        )

    def filt_copy(k):
        return pltpu.make_async_remote_copy(
            src_ref=filt_s, dst_ref=filt_r.at[me], send_sem=filt_sem.at[0], recv_sem=filt_sem.at[1],
            device_id={"ctx": peer(k)}, device_id_type=MESH,
        )

    for k in range(n - 1):
        filt_copy(k).start()

    order = [(c + chunks // 2) % chunks for c in range(chunks)]

    @pl.when(has_right)
    def _():
        rim_copy.start()
        for c in order:
            ph_copy(c).start()

    @pl.when(has_left)
    def _():
        col_copy.start()
        for c in order:
            gh_copy(c).start()

    for load in loads[8:]:
        load.wait()

    def forward_rows(t, carry):
        turned = []
        for u in range(4):
            rows = pl.ds(pl.multiple_of(t * 64 + u * GROUP, GROUP), GROUP)
            taps3 = [tap_of(w, rows) for w in range(3)]
            b1, b2 = [None] * 3, [None] * 3
            for i in range(blocks):
                short = [None] * 3
                for w, src in enumerate((qx, kx, vx)):
                    if i == last and w > 0:
                        continue
                    x = src[rows, lanes(i)]
                    r1, r2 = pltpu.roll(x, 1, 1), pltpu.roll(x, 2, 1)
                    if i > 0 or w > 0:
                        short[w] = short_forward(w, rows, i, taps3[w], x, r1, r2, b1[w], b2[w])
                    b1[w], b2[w] = r1, r2
                if i < last:
                    kc[rows, lanes(i)] = short[1]
                    vc[rows, lanes(i)] = short[2]
                    pr[rows, lanes(i)] = short[1] * short[2]
                if i > 0:
                    m = gx[rows, lanes(i)] * short[0]
                    gm[rows, lanes(i)] = m
                    turned.append(m)
        turned = nn(jnp.concatenate(turned, axis=0), flip).astype(BF)
        for u in range(4):
            rows = pl.ds(pl.multiple_of(t * 64 + u * GROUP, GROUP), GROUP)
            for i in range(1, blocks):
                at = (u * last + i - 1) * GROUP
                gmr[rows, lanes(i)] = turned[at : at + GROUP]
        return carry

    lax.fori_loop(0, channels // 64, forward_rows, 0)

    @pl.when(has_left)
    def _():
        rim_copy.wait_recv()

    @pl.when(jnp.logical_not(has_left))
    def _():
        rim_r[...] = jnp.zeros(rim_r.shape, F32)
        ph[...] = jnp.zeros(ph.shape, BF)

    @pl.when(has_right)
    def _():
        col_copy.wait_recv()

    @pl.when(jnp.logical_not(has_right))
    def _():
        col_r[...] = jnp.zeros(col_r.shape, F32)
        edge_r[...] = jnp.zeros(edge_r.shape, F32)
        gh[...] = jnp.zeros(gh.shape, BF)

    def drain(ref, sem):
        pltpu.make_async_copy(ref, ref, sem).wait()

    others = pl.ds(0, n - 1)
    drain(filt_r.at[others], filt_sem.at[1])

    sq_row, sq_col = iota((LANE, LANE), 0), iota((LANE, LANE), 1)
    upper = sq_col >= sq_row
    early = sq_col + sq_row <= LANE - 1
    zero_sq = jnp.zeros((LANE, LANE), BF)
    rim_place = place((0, 0, 0, 0))
    pad = jnp.zeros((GROUP, LANE), BF)

    def shift_left(cur, after, mask):
        return jnp.where(mask, zero16 if after is None else after, cur)

    def msg_copy(o):
        return pltpu.make_async_remote_copy(
            src_ref=msg_s.at[o], dst_ref=msg_r.at[me], send_sem=msg_sem.at[0], recv_sem=msg_sem.at[1],
            device_id={"ctx": o}, device_id_type=MESH,
        )

    def halo_ready(base):
        for c in range(chunks):
            @pl.when(base == c * part)
            def _():
                @pl.when(has_left)
                def _():
                    ph_copy(c).wait_recv()

                @pl.when(has_right)
                def _():
                    gh_copy(c).wait_recv()

    def rims_in(t):
        cols = pl.ds(pl.multiple_of(t * TILE, TILE), TILE)
        rim, own, far = rim_r[:, cols], rim_s[:, cols], col_r[:, cols]
        rows = []
        for w in range(3):
            tap1, tap2 = taps[w, 1:2, cols], taps[w, 2:3, cols]
            x2, x1 = rim[2 * w : 2 * w + 1], rim[2 * w + 1 : 2 * w + 2]
            rows += [tap1 * x1 + tap2 * x2, tap2 * x1]
        tap1, tap2 = taps[0, 1:2, cols], taps[0, 2:3, cols]
        rows += [far[0:1] * (tap1 * own[1:2] + tap2 * own[0:1]), far[1:2] * (tap2 * own[1:2])]
        rows.append(jnp.zeros((8, TILE), F32))
        fix = tn(jnp.concatenate(rows, axis=0).astype(BF), rim_place).astype(BF)
        kk = kc[cols, lanes(0)] + fix[:, LANE : 2 * LANE]
        vv = vc[cols, lanes(0)] + fix[:, 2 * LANE : 3 * LANE]
        kc[cols, lanes(0)] = kk
        vc[cols, lanes(0)] = vv
        pr[cols, lanes(0)] = kk * vv
        m0 = gm[cols, lanes(0)] + gx[cols, lanes(0)] * fix[:, :LANE]
        first[cols, :] = m0
        gmr[cols, lanes(0)] = nn(m0, flip).astype(BF)
        after[cols, :] = gh[cols, :] + fix[:, 3 * LANE :]
        bias_b[cols, :] = spread(
            filt_r[t * 4, 2:3, :] + filt_r[t * 4 + 1, 2:3, :]
            + filt_r[t * 4 + 2, 2:3, :] + filt_r[t * 4 + 3, 2:3, :]
        )

    depth = blocks * GROUP

    def matmuls(t, u):
        rows = pl.ds(pl.multiple_of(t * TILE + u * GROUP, GROUP), GROUP)
        slot = t * 4 + u // 2
        filt = filt_r[slot, u % 2 : u % 2 + 1, :].astype(BF)
        round_filt = pltpu.roll(jnp.broadcast_to(filt, (LANE, LANE)), 0, 1, stride=1, stride_axis=0)
        now = jnp.where(upper, round_filt, zero_sq)
        then = jnp.where(upper, zero_sq, round_filt)
        p = [ph[rows, :]] + [pr[rows, lanes(i)] for i in range(blocks)]
        m = [first[rows, :]] + [gm[rows, lanes(i)] for i in range(1, blocks)] + [after[rows, :]]
        p_ext = jnp.concatenate(p, axis=0)
        m_ext = jnp.concatenate(m, axis=0)
        conv[u % 2, 0] = nn(
            jnp.concatenate([p_ext[:depth], p_ext[GROUP:]], axis=1),
            jnp.concatenate([then, now], axis=0),
        ).astype(BF)
        conv[u % 2, 1] = nt(
            jnp.concatenate([m_ext[:depth], m_ext[GROUP:]], axis=1),
            jnp.concatenate([now, then], axis=1),
        ).astype(BF)
        m_rev = [gmr[rows, lanes(i)] for i in range(blocks)]
        diff = tn(
            p_ext,
            jnp.concatenate(
                [jnp.concatenate(m_rev + [pad], axis=0), jnp.concatenate([pad] + m_rev, axis=0)], axis=1
            ),
        )
        diff = jnp.where(early, diff[:, LANE:], diff[:, :LANE]).astype(BF)
        diff = pltpu.roll(diff, 0, 1, stride=1, stride_axis=0)
        msg_s[slot, u % 2 : u % 2 + 1, :] = jnp.sum(diff.astype(F32), axis=0, keepdims=True)

    def gradients(t, u):
        rows = pl.ds(pl.multiple_of(t * TILE + u * GROUP, GROUP), GROUP)
        own_rows = pl.ds(u * GROUP, GROUP)
        bias = bias_b[rows, :]
        bias_sum = None
        gw = [[None] * blocks for _ in range(3)]
        for i in range(blocks):
            p = pr[rows, lanes(i)]
            m = first[rows, :] if i == 0 else gm[rows, lanes(i)]
            mixed = conv[u % 2, 0, pl.ds(i * GROUP, GROUP), :] + bias * p
            back = conv[u % 2, 1, pl.ds(i * GROUP, GROUP), :] + bias * m
            gw[0][i] = gx[rows, lanes(i)] * mixed
            gw[1][i] = back * vc[rows, lanes(i)]
            gw[2][i] = back * kc[rows, lanes(i)]
            term = m * p
            bias_sum = term if bias_sum is None else bias_sum + term
        acc[lax.rem(t, 2), 9, own_rows, :] = bias_sum
        for w, src in enumerate((qx, kx, vx)):
            sums = [None] * SHORT
            for i in range(blocks):
                g0 = gw[w][i]
                raw[w, rows, lanes(i)] = g0
                for j in range(SHORT):
                    x = src[rows, lanes(i)] if j == 0 else xs[w, j - 1, rows, lanes(i)]
                    sums[j] = g0 * x if sums[j] is None else sums[j] + g0 * x
            for j in range(SHORT):
                acc[lax.rem(t, 2), w * 3 + j, own_rows, :] = sums[j]
            heads[lax.rem(t, 2), w, own_rows, :] = gw[w][0]

    halves = ((iota((8, 2 * LANE), 1) // LANE) == iota((8, 2 * LANE), 0)).astype(F32).astype(BF)

    def lane_sums(a, b, c, d):
        sums = nt(
            halves,
            jnp.concatenate(
                [jnp.concatenate([a, b], axis=1), jnp.concatenate([c, d], axis=1)], axis=0
            ),
        )
        return [sums[0:1, :LANE], sums[1:2, :LANE], sums[0:1, LANE:], sums[1:2, LANE:]]

    def tile_sums(t):
        cols = pl.ds(pl.multiple_of(t * TILE, TILE), TILE)
        k = lax.rem(t, 2)
        edge = (
            nt(pick(0, 0), heads[k, 0]) + nt(pick(1, 0), heads[k, 1]) + nt(pick(2, 0), heads[k, 2])
        )
        edge_s[:, cols] = edge
        rim = rim_r[:, cols]
        sums = lane_sums(acc[k, 0], acc[k, 1], acc[k, 2], acc[k, 3])
        sums += lane_sums(acc[k, 4], acc[k, 5], acc[k, 6], acc[k, 7])
        sums += lane_sums(acc[k, 8], acc[k, 9], acc[k, 8], acc[k, 9])
        blank = jnp.zeros((2, LANE), F32)
        for w in range(3):
            g0, g1 = edge[2 * w : 2 * w + 1], edge[2 * w + 1 : 2 * w + 2]
            x2, x1 = rim[2 * w : 2 * w + 1], rim[2 * w + 1 : 2 * w + 2]
            row1 = sums[w * 3 + 1] + g0 * x1
            row2 = sums[w * 3 + 2] + g0 * x2 + g1 * x1
            msg_s[t * 4 + w, 2:8, :] = jnp.concatenate([sums[9], sums[w * 3], row1, row2, blank], axis=0)
        msg_s[t * 4 + 3, 2:8, :] = jnp.concatenate([sums[9], blank, blank, blank[:1]], axis=0)

    def send_sums(t):
        for i in range(4):
            o = t * 4 + i

            @pl.when(o != me)
            def _():
                msg_copy(o).start()

    def main_tile(step, before, ahead):
        t = tile_at(step)
        if ahead:
            halo_ready(tile_at(step + 1) * TILE)
        groups = TILE // GROUP
        matmuls(t, 0)
        if before:
            tile_sums(tile_at(step - 1))
        for u in range(groups):
            if u + 1 < groups:
                matmuls(t, u + 1)
            if ahead and u == 2:
                rims_in(tile_at(step + 1))
            gradients(t, u)
        if before:
            send_sums(tile_at(step - 1))

    def tile_at(step):
        return (step + tiles // 2) % tiles

    def middle_tile(step, carry):
        main_tile(step, True, True)
        return carry

    halo_ready(tile_at(0) * TILE)
    rims_in(tile_at(0))
    main_tile(0, False, True)
    lax.fori_loop(1, tiles - 1, middle_tile, 0)
    main_tile(tiles - 1, True, False)
    tile_sums(tile_at(tiles - 1))
    send_sums(tile_at(tiles - 1))

    edge_copy = pltpu.make_async_remote_copy(
        src_ref=edge_s, dst_ref=edge_r, send_sem=edge_sem.at[0], recv_sem=edge_sem.at[1],
        device_id={"ctx": left}, device_id_type=MESH,
    )

    @pl.when(has_left)
    def _():
        edge_copy.start()

    def output_rows(t):
        for u in range(4):
            rows = pl.ds(pl.multiple_of(t * 64 + u * GROUP, GROUP), GROUP)
            for w, dst in enumerate((out_q, out_k, out_v)):
                tap = tap_of(w, rows)
                a1 = a2 = None
                for i in reversed(range(blocks)):
                    g0 = raw[w, rows, lanes(i)]
                    r1, r2 = pltpu.roll(g0, LANE - 1, 1), pltpu.roll(g0, LANE - 2, 1)
                    dst[rows, lanes(i)] = (
                        tap[0] * g0 + tap[1] * shift_left(r1, a1, last1) + tap[2] * shift_left(r2, a2, last2)
                    )
                    a1, a2 = r1, r2

    def output_loop(t, carry):
        output_rows(t)
        return carry

    lax.fori_loop(0, tiles, output_loop, 0)

    msg_r[me] = msg_s[me]
    drain(msg_r.at[others], msg_sem.at[1])

    total = msg_r[0]
    for o in range(1, n):
        total = total + msg_r[o]
    tot_s[...] = jnp.concatenate([total[3:6], jnp.zeros((5, LANE), F32)], axis=0)

    def tot_copy(k):
        return pltpu.make_async_remote_copy(
            src_ref=tot_s, dst_ref=tot_r.at[me], send_sem=tot_sem.at[0], recv_sem=tot_sem.at[1],
            device_id={"ctx": peer(k)}, device_id_type=MESH,
        )

    for k in range(3):
        tot_copy(k).start()

    def output_and_send(t, carry):
        for k in range(4):
            tot_copy(4 * t + 3 + k).start()
        output_rows(t + tiles)
        return carry

    lax.fori_loop(0, tiles - 1, output_and_send, 0)
    output_rows(2 * tiles - 1)
    tot_r[me] = tot_s[...]
    out_filt[...] = lax.dot_general(
        total, flip.astype(F32), (((1,), (0,)), ((), ())),
        preferred_element_type=F32, precision=lax.Precision.HIGHEST,
    )[0:2]
    out_bias[...] = pltpu.roll(total[2:3], lax.rem(LANE - lax.rem(me, 4) * 32, LANE), 1)

    @pl.when(has_right)
    def _():
        edge_copy.wait_recv()

    out_edge[...] = edge_r[...]

    drain(filt_r.at[others], filt_sem.at[0])
    drain(msg_r.at[others], msg_sem.at[0])

    @pl.when(has_right)
    def _():
        rim_copy.wait_send()
        for c in range(chunks):
            ph_copy(c).wait_send()

    @pl.when(has_left)
    def _():
        col_copy.wait_send()
        edge_copy.wait_send()
        for c in range(chunks):
            gh_copy(c).wait_send()

    drain(tot_r.at[others], tot_sem.at[1])
    for w in range(3):
        for t in range(tiles):
            out_short[w, :, t * TILE : (t + 1) * TILE] = tot_r[t * 4 + w, 0:SHORT, :]
    drain(tot_r.at[others], tot_sem.at[0])


def finish(
    blocks,
    gq, gk, gv, edge, short, filt, bias, taps_hbm,
    out_q, out_k, out_v, out_short, out_filt, out_bias,
    taps, ends, bias_v, sem, end_sem,
):
    last = blocks - 1
    bulk = pl.ds(0, last * LANE)
    copies = [pltpu.make_async_copy(taps_hbm, taps, sem.at[0])]
    for i, (src, dst) in enumerate(((gq, out_q), (gk, out_k), (gv, out_v))):
        copies.append(pltpu.make_async_copy(src.at[:, bulk], dst.at[:, bulk], sem.at[1 + i]))
    copies.append(pltpu.make_async_copy(short, out_short, sem.at[4]))
    copies.append(pltpu.make_async_copy(filt, out_filt, sem.at[5]))
    for copy in copies:
        copy.start()
    bias_v[...] = bias[0, : bias_v.shape[0]]
    copies.append(pltpu.make_async_copy(bias_v, out_bias, sem.at[6]))
    copies[-1].start()
    copies[0].wait()
    rim_place = place((LANE - 2, LANE - 2, LANE - 2))
    for t in range(gq.shape[0] // TILE):
        cols = pl.ds(t * TILE, TILE)
        x = edge[:, cols]
        rows = []
        for w in range(3):
            tap1, tap2 = taps[w, 1:2, cols], taps[w, 2:3, cols]
            g0, g1 = x[2 * w : 2 * w + 1], x[2 * w + 1 : 2 * w + 2]
            rows += [tap2 * g0, tap1 * g0 + tap2 * g1]
        rows.append(jnp.zeros((10, TILE), F32))
        fix = tn(jnp.concatenate(rows, axis=0).astype(BF), rim_place).astype(BF)
        for w, src in enumerate((gq, gk, gv)):
            ends[w, cols, :] = src[cols, lanes(last)] + fix[:, w * LANE : (w + 1) * LANE]
    for w, dst in enumerate((out_q, out_k, out_v)):
        copies.append(pltpu.make_async_copy(ends.at[w], dst.at[:, lanes(last)], end_sem.at[w]))
        copies[-1].start()
    for copy in copies[1:]:
        copy.wait()


def body(query_feat, key_feat, value_feat, grad_out, short_taps, filters, skip_bias):
    channels, length = query_feat.shape
    n = lax.axis_size("ctx")
    blocks = length // LANE
    full, tile = (channels, length), (channels, LANE)
    vmem = pl.BlockSpec(memory_space=pltpu.VMEM)
    hbm = pl.BlockSpec(memory_space=pltpu.HBM)
    dma = pltpu.SemaphoreType.DMA
    row = pltpu.VMEM((8, channels), F32)
    slots = pltpu.VMEM((n, 8, LANE), F32)
    one = pltpu.VMEM((8, LANE), F32)
    short_taps, filters, skip_bias = [
        pltpu.with_memory_space_constraint(x, pltpu.HBM) for x in (short_taps, filters, skip_bias)
    ]
    outs = pl.pallas_call(
        functools.partial(kernel, n, blocks),
        out_shape=(
            pltpu.VMEM(full, BF), pltpu.VMEM(full, BF), pltpu.VMEM(full, BF),
            row,
            pltpu.VMEM(short_taps.shape, F32),
            pltpu.VMEM(filters.shape, F32),
            pltpu.VMEM((1, LANE), F32),
        ),
        in_specs=[hbm] * 7,
        out_specs=(vmem,) * 7,
        scratch_shapes=[pltpu.VMEM(full, BF)] * 9
        + [
            pltpu.VMEM((3, channels, length), BF),
            pltpu.VMEM((3, 2, channels, length), BF),
            pltpu.VMEM((2, 2, blocks * GROUP, LANE), BF),
            pltpu.VMEM((2, 10, TILE, LANE), BF),
            pltpu.VMEM((2, 3, TILE, LANE), BF),
            pltpu.VMEM(tile, BF), pltpu.VMEM(tile, BF),
            pltpu.VMEM(tile, BF), pltpu.VMEM(tile, BF),
            pltpu.VMEM(short_taps.shape, F32),
            pltpu.VMEM(filters.shape, BF),
            pltpu.VMEM(skip_bias.shape, BF),
            pltpu.VMEM((9, channels, LANE), BF),
            pltpu.VMEM(tile, BF),
            row, row, row, row, one, slots, slots, slots, one, slots, row, row,
            dma((12,)), dma((2,)), dma((2,)),
            dma((CHUNKS,)), dma((CHUNKS,)), dma((CHUNKS,)), dma((CHUNKS,)),
            dma((2,)), dma((2,)), dma((2,)), dma((2,)),
        ],
        compiler_params=pltpu.CompilerParams(
            collective_id=0, has_side_effects=True, vmem_limit_bytes=48 * 1024 * 1024
        ),
    )(query_feat, key_feat, value_feat, grad_out, short_taps, filters, skip_bias)
    return pl.pallas_call(
        functools.partial(finish, blocks),
        out_shape=tuple(
            jax.ShapeDtypeStruct(s, d)
            for s, d in (
                (full, BF), (full, BF), (full, BF),
                (short_taps.shape, F32), (filters.shape, F32), (skip_bias.shape, F32),
            )
        ),
        in_specs=[vmem] * 7 + [hbm],
        out_specs=(hbm,) * 6,
        scratch_shapes=[
            pltpu.VMEM(short_taps.shape, F32),
            pltpu.VMEM((3,) + tile, BF),
            pltpu.VMEM(skip_bias.shape, F32),
            dma((7,)), dma((3,)),
        ],
        compiler_params=pltpu.CompilerParams(vmem_limit_bytes=16 * 1024 * 1024),
    )(*outs, short_taps)


def solution(mesh):
    wide, narrow = P("tp", "ctx"), P(None, None, "tp")
    both = ("tp", "ctx")

    def whole(*args):
        with jax.sharding.use_abstract_mesh(mesh.abstract_mesh):
            return jax.shard_map(
                body,
                mesh=mesh,
                in_specs=(wide, wide, wide, wide, narrow, P(both, None), P(both)),
                out_specs=(wide, wide, wide, narrow, P(both, None), P(both)),
                check_vma=False,
            )(*args)

    return whole
```

```python
import functools

import jax
import jax.numpy as jnp
from jax import lax
from jax.experimental import pallas as pl
from jax.experimental.pallas import tpu as pltpu
from jax.sharding import PartitionSpec as P

TAPS = 128
SHORT = 3
GROUP = 16
LANE = 128
TILE = 128
CHUNKS = 4
BF = jnp.bfloat16
F32 = jnp.float32
MESH = pl.DeviceIdType.MESH


def nn(a, b):
    return lax.dot_general(a, b, (((1,), (0,)), ((), ())), preferred_element_type=F32)


def nt(a, b):
    return lax.dot_general(a, b, (((1,), (1,)), ((), ())), preferred_element_type=F32)


def tn(a, b):
    return lax.dot_general(a, b, (((0,), (0,)), ((), ())), preferred_element_type=F32)


def iota(shape, axis):
    return lax.broadcasted_iota(jnp.int32, shape, axis)


def lanes(i):
    return pl.ds(i * LANE, LANE)


def place(firsts):
    sub, lane = iota((16, LANE), 0), iota((16, LANE), 1)
    blocks = [
        ((sub // 2 == w) & (lane == first + sub % 2)).astype(F32).astype(BF)
        for w, first in enumerate(firsts)
    ]
    return jnp.concatenate(blocks, axis=1)


def kernel(
    n, blocks,
    q_hbm, k_hbm, v_hbm, g_hbm, taps_hbm, filt_hbm, bias_hbm,
    out_q, out_k, out_v, out_edge, out_short, out_filt, out_bias,
    qx, kx, vx, gx, kc, vc, pr, gm, gmr, raw, xs, conv, acc, heads, first, after, ph, gh, taps, filt_in, bias_in, taps_b, bias_b,
    rim_s, rim_r, col_s, col_r, filt_s, filt_r, msg_s, msg_r, tot_s, tot_r, edge_s, edge_r,
    in_sem, rim_sem, col_sem, ph_ssem, ph_rsem, gh_ssem, gh_rsem, filt_sem, msg_sem, tot_sem, edge_sem,
):
    me = lax.axis_index("ctx")
    channels = qx.shape[0]
    tiles = channels // TILE
    chunks = min(CHUNKS, tiles)
    last = blocks - 1
    part = channels // chunks
    right, left = lax.rem(me + 1, n), lax.rem(me + n - 1, n)
    has_left, has_right = me > 0, me < n - 1

    def peer(k):
        if n != 32:
            return lax.rem(me + 1 + k, n)
        i, j = k // 8, k // 2 % 4
        dz = 1 + 2 * i - 3 * (i // 2)
        dx = 2 - j + 3 * (j // 2) + 2 * (j // 3)
        z, x, c = (me // 8 + dz) % 4, (me // 2 + dx) % 4, (me + 1 + k % 2) % 2
        return z * 8 + x * 2 + c

    def piece(i, src, dst, start, size):
        cols = pl.ds(start * LANE, size * LANE)
        return pltpu.make_async_copy(src.at[:, cols], dst.at[:, cols], in_sem.at[i])

    loads = [
        pltpu.make_async_copy(taps_hbm, taps, in_sem.at[0]),
        pltpu.make_async_copy(filt_hbm, filt_in, in_sem.at[1]),
        pltpu.make_async_copy(bias_hbm, bias_in, in_sem.at[2]),
        piece(3, k_hbm, kx, blocks - 2, 2),
        piece(4, v_hbm, vx, blocks - 2, 2),
        piece(5, q_hbm, qx, last, 1),
        piece(6, q_hbm, qx, 0, 1),
        piece(7, g_hbm, gx, 0, 1),
        piece(8, k_hbm, kx, 0, blocks - 2),
        piece(9, v_hbm, vx, 0, blocks - 2),
        piece(10, q_hbm, qx, 1, blocks - 2),
        piece(11, g_hbm, gx, 1, blocks - 1),
    ]
    for load in loads:
        load.start()

    barrier = pltpu.get_barrier_semaphore()

    def greet(d, carry):
        pl.semaphore_signal(
            barrier, inc=1, device_id={"ctx": lax.rem(me + d, n)}, device_id_type=MESH
        )
        return carry

    lax.fori_loop(1, n, greet, 0)

    lane16 = iota((GROUP, LANE), 1)
    first1, first2 = lane16 < 1, lane16 < 2
    last1, last2 = lane16 >= LANE - 1, lane16 >= LANE - 2
    zero16 = jnp.zeros((GROUP, LANE), BF)
    eye = iota((TILE, TILE), 0) == iota((TILE, TILE), 1)
    ones = jnp.ones((TILE, LANE), BF)
    flip = (iota((LANE, LANE), 0) + iota((LANE, LANE), 1) == LANE - 1).astype(F32).astype(BF)

    def spread(row):
        return nn(jnp.where(eye, row, 0.0).astype(BF), ones).astype(BF)

    def tap_tile(t):
        cols = pl.ds(pl.multiple_of(t * TILE, TILE), TILE)
        for w in range(3):
            for j in range(SHORT):
                taps_b[w * 3 + j, cols, :] = spread(taps[w, j : j + 1, cols])

    loads[0].wait()
    tap_tile(0)

    loads[1].wait()
    loads[2].wait()
    own_bias = bias_in[...].astype(F32).reshape(1, -1)
    own_bias = jnp.pad(own_bias, ((0, 0), (0, LANE - own_bias.shape[1])))
    own_bias = pltpu.roll(own_bias, lax.rem(me, 4) * 32, 1)
    filt_s[...] = jnp.concatenate(
        [filt_in[...].astype(F32), own_bias, jnp.zeros((5, LANE), F32)], axis=0
    )
    filt_r[me] = filt_s[...]

    sub8, lane8 = iota((8, LANE), 0), iota((8, LANE), 1)

    def pick(w, first_lane):
        return ((sub8 // 2 == w) & (lane8 == first_lane + sub8 % 2)).astype(F32).astype(BF)

    def shift_right(cur, before, mask):
        return jnp.where(mask, zero16 if before is None else before, cur)

    def short_forward(w, rows, i, tap, x, r1, r2, b1, b2):
        s1, s2 = shift_right(r1, b1, first1), shift_right(r2, b2, first2)
        xs[w, 0, rows, lanes(i)] = s1
        xs[w, 1, rows, lanes(i)] = s2
        return tap[0] * x + tap[1] * s1 + tap[2] * s2

    for load in loads[3:8]:
        load.wait()
    rim_s[...] = (
        nt(pick(0, LANE - 2), qx[:, lanes(last)])
        + nt(pick(1, LANE - 2), kx[:, lanes(last)])
        + nt(pick(2, LANE - 2), vx[:, lanes(last)])
    )
    col_s[...] = nt(pick(0, 0), gx[:, lanes(0)])

    def tap_of(w, rows):
        return [taps_b[w * 3 + j, rows, :] for j in range(SHORT)]

    def border_tile(t):
        for u in range(TILE // GROUP):
            rows = pl.ds(pl.multiple_of(t * TILE + u * GROUP, GROUP), GROUP)
            kv = []
            for w, (src, dst) in ((1, (kx, kc)), (2, (vx, vc))):
                x, prev = src[rows, lanes(last)], src[rows, lanes(last - 1)]
                y = short_forward(
                    w, rows, last, tap_of(w, rows), x, pltpu.roll(x, 1, 1), pltpu.roll(x, 2, 1),
                    pltpu.roll(prev, 1, 1), pltpu.roll(prev, 2, 1),
                )
                dst[rows, lanes(last)] = y
                kv.append(y)
            pr[rows, lanes(last)] = kv[0] * kv[1]
            x = qx[rows, lanes(0)]
            y = short_forward(
                0, rows, 0, tap_of(0, rows), x, pltpu.roll(x, 1, 1), pltpu.roll(x, 2, 1), None, None
            )
            gm[rows, lanes(0)] = gx[rows, lanes(0)] * y

    def start_tile(t, carry):
        tap_tile(t)
        border_tile(t - 1)
        return carry

    lax.fori_loop(1, tiles, start_tile, 0)
    border_tile(tiles - 1)

    pl.semaphore_wait(barrier, n - 1)

    rim_copy = pltpu.make_async_remote_copy(
        src_ref=rim_s, dst_ref=rim_r, send_sem=rim_sem.at[0], recv_sem=rim_sem.at[1],
        device_id={"ctx": right}, device_id_type=MESH,
    )
    col_copy = pltpu.make_async_remote_copy(
        src_ref=col_s, dst_ref=col_r, send_sem=col_sem.at[0], recv_sem=col_sem.at[1],
        device_id={"ctx": left}, device_id_type=MESH,
    )

    def ph_copy(c):
        rows = pl.ds(c * part, part)
        return pltpu.make_async_remote_copy(
            src_ref=pr.at[rows, lanes(last)], dst_ref=ph.at[rows, :],
            send_sem=ph_ssem.at[c], recv_sem=ph_rsem.at[c],
            device_id={"ctx": right}, device_id_type=MESH,
        )

    def gh_copy(c):
        rows = pl.ds(c * part, part)
        return pltpu.make_async_remote_copy(
            src_ref=gm.at[rows, lanes(0)], dst_ref=gh.at[rows, :],
            send_sem=gh_ssem.at[c], recv_sem=gh_rsem.at[c],
            device_id={"ctx": left}, device_id_type=MESH,
        )

    def filt_copy(k):
        return pltpu.make_async_remote_copy(
            src_ref=filt_s, dst_ref=filt_r.at[me], send_sem=filt_sem.at[0], recv_sem=filt_sem.at[1],
            device_id={"ctx": peer(k)}, device_id_type=MESH,
        )

    for k in range(n - 1):
        filt_copy(k).start()

    order = [(c + chunks // 2) % chunks for c in range(chunks)]

    @pl.when(has_right)
    def _():
        rim_copy.start()
        for c in order:
            ph_copy(c).start()

    @pl.when(has_left)
    def _():
        col_copy.start()
        for c in order:
            gh_copy(c).start()

    for load in loads[8:]:
        load.wait()

    def forward_rows(t, carry):
        turned = []
        for u in range(8):
            rows = pl.ds(pl.multiple_of(t * 128 + u * GROUP, GROUP), GROUP)
            taps3 = [tap_of(w, rows) for w in range(3)]
            b1, b2 = [None] * 3, [None] * 3
            for i in range(blocks):
                short = [None] * 3
                for w, src in enumerate((qx, kx, vx)):
                    if i == last and w > 0:
                        continue
                    x = src[rows, lanes(i)]
                    r1, r2 = pltpu.roll(x, 1, 1), pltpu.roll(x, 2, 1)
                    if i > 0 or w > 0:
                        short[w] = short_forward(w, rows, i, taps3[w], x, r1, r2, b1[w], b2[w])
                    b1[w], b2[w] = r1, r2
                if i < last:
                    kc[rows, lanes(i)] = short[1]
                    vc[rows, lanes(i)] = short[2]
                    pr[rows, lanes(i)] = short[1] * short[2]
                if i > 0:
                    m = gx[rows, lanes(i)] * short[0]
                    gm[rows, lanes(i)] = m
                    turned.append(m)
        turned = nn(jnp.concatenate(turned, axis=0), flip).astype(BF)
        for u in range(8):
            rows = pl.ds(pl.multiple_of(t * 128 + u * GROUP, GROUP), GROUP)
            for i in range(1, blocks):
                at = (u * last + i - 1) * GROUP
                gmr[rows, lanes(i)] = turned[at : at + GROUP]
        return carry

    lax.fori_loop(0, channels // 128, forward_rows, 0)

    @pl.when(has_left)
    def _():
        rim_copy.wait_recv()

    @pl.when(jnp.logical_not(has_left))
    def _():
        rim_r[...] = jnp.zeros(rim_r.shape, F32)
        ph[...] = jnp.zeros(ph.shape, BF)

    @pl.when(has_right)
    def _():
        col_copy.wait_recv()

    @pl.when(jnp.logical_not(has_right))
    def _():
        col_r[...] = jnp.zeros(col_r.shape, F32)
        edge_r[...] = jnp.zeros(edge_r.shape, F32)
        gh[...] = jnp.zeros(gh.shape, BF)

    def drain(ref, sem):
        pltpu.make_async_copy(ref, ref, sem).wait()

    others = pl.ds(0, n - 1)
    drain(filt_r.at[others], filt_sem.at[1])

    sq_row, sq_col = iota((LANE, LANE), 0), iota((LANE, LANE), 1)
    upper = sq_col >= sq_row
    early = sq_col + sq_row <= LANE - 1
    zero_sq = jnp.zeros((LANE, LANE), BF)
    rim_place = place((0, 0, 0, 0))
    pad = jnp.zeros((GROUP, LANE), BF)

    def shift_left(cur, after, mask):
        return jnp.where(mask, zero16 if after is None else after, cur)

    def msg_copy(o):
        return pltpu.make_async_remote_copy(
            src_ref=msg_s.at[o], dst_ref=msg_r.at[me], send_sem=msg_sem.at[0], recv_sem=msg_sem.at[1],
            device_id={"ctx": o}, device_id_type=MESH,
        )

    def halo_ready(base):
        for c in range(chunks):
            @pl.when(base == c * part)
            def _():
                @pl.when(has_left)
                def _():
                    ph_copy(c).wait_recv()

                @pl.when(has_right)
                def _():
                    gh_copy(c).wait_recv()

    def rims_in(t):
        cols = pl.ds(pl.multiple_of(t * TILE, TILE), TILE)
        rim, own, far = rim_r[:, cols], rim_s[:, cols], col_r[:, cols]
        rows = []
        for w in range(3):
            tap1, tap2 = taps[w, 1:2, cols], taps[w, 2:3, cols]
            x2, x1 = rim[2 * w : 2 * w + 1], rim[2 * w + 1 : 2 * w + 2]
            rows += [tap1 * x1 + tap2 * x2, tap2 * x1]
        tap1, tap2 = taps[0, 1:2, cols], taps[0, 2:3, cols]
        rows += [far[0:1] * (tap1 * own[1:2] + tap2 * own[0:1]), far[1:2] * (tap2 * own[1:2])]
        rows.append(jnp.zeros((8, TILE), F32))
        fix = tn(jnp.concatenate(rows, axis=0).astype(BF), rim_place).astype(BF)
        kk = kc[cols, lanes(0)] + fix[:, LANE : 2 * LANE]
        vv = vc[cols, lanes(0)] + fix[:, 2 * LANE : 3 * LANE]
        kc[cols, lanes(0)] = kk
        vc[cols, lanes(0)] = vv
        pr[cols, lanes(0)] = kk * vv
        m0 = gm[cols, lanes(0)] + gx[cols, lanes(0)] * fix[:, :LANE]
        first[cols, :] = m0
        gmr[cols, lanes(0)] = nn(m0, flip).astype(BF)
        after[cols, :] = gh[cols, :] + fix[:, 3 * LANE :]
        bias_b[cols, :] = spread(
            filt_r[t * 4, 2:3, :] + filt_r[t * 4 + 1, 2:3, :]
            + filt_r[t * 4 + 2, 2:3, :] + filt_r[t * 4 + 3, 2:3, :]
        )

    depth = blocks * GROUP

    def matmuls(t, u):
        rows = pl.ds(pl.multiple_of(t * TILE + u * GROUP, GROUP), GROUP)
        slot = t * 4 + u // 2
        filt = filt_r[slot, u % 2 : u % 2 + 1, :].astype(BF)
        round_filt = pltpu.roll(jnp.broadcast_to(filt, (LANE, LANE)), 0, 1, stride=1, stride_axis=0)
        now = jnp.where(upper, round_filt, zero_sq)
        then = jnp.where(upper, zero_sq, round_filt)
        p = [ph[rows, :]] + [pr[rows, lanes(i)] for i in range(blocks)]
        m = [first[rows, :]] + [gm[rows, lanes(i)] for i in range(1, blocks)] + [after[rows, :]]
        p_ext = jnp.concatenate(p, axis=0)
        m_ext = jnp.concatenate(m, axis=0)
        conv[u % 2, 0] = nn(
            jnp.concatenate([p_ext[:depth], p_ext[GROUP:]], axis=1),
            jnp.concatenate([then, now], axis=0),
        ).astype(BF)
        conv[u % 2, 1] = nt(
            jnp.concatenate([m_ext[:depth], m_ext[GROUP:]], axis=1),
            jnp.concatenate([now, then], axis=1),
        ).astype(BF)
        m_rev = [gmr[rows, lanes(i)] for i in range(blocks)]
        diff = tn(
            p_ext,
            jnp.concatenate(
                [jnp.concatenate(m_rev + [pad], axis=0), jnp.concatenate([pad] + m_rev, axis=0)], axis=1
            ),
        )
        diff = jnp.where(early, diff[:, LANE:], diff[:, :LANE]).astype(BF)
        diff = pltpu.roll(diff, 0, 1, stride=1, stride_axis=0)
        msg_s[slot, u % 2 : u % 2 + 1, :] = jnp.sum(diff.astype(F32), axis=0, keepdims=True)

    def gradients(t, u):
        rows = pl.ds(pl.multiple_of(t * TILE + u * GROUP, GROUP), GROUP)
        own_rows = pl.ds(u * GROUP, GROUP)
        bias = bias_b[rows, :]
        bias_sum = None
        gw = [[None] * blocks for _ in range(3)]
        for i in range(blocks):
            p = pr[rows, lanes(i)]
            m = first[rows, :] if i == 0 else gm[rows, lanes(i)]
            mixed = conv[u % 2, 0, pl.ds(i * GROUP, GROUP), :] + bias * p
            back = conv[u % 2, 1, pl.ds(i * GROUP, GROUP), :] + bias * m
            gw[0][i] = gx[rows, lanes(i)] * mixed
            gw[1][i] = back * vc[rows, lanes(i)]
            gw[2][i] = back * kc[rows, lanes(i)]
            term = m * p
            bias_sum = term if bias_sum is None else bias_sum + term
        acc[lax.rem(t, 2), 9, own_rows, :] = bias_sum
        for w, src in enumerate((qx, kx, vx)):
            sums = [None] * SHORT
            for i in range(blocks):
                g0 = gw[w][i]
                raw[w, rows, lanes(i)] = g0
                for j in range(SHORT):
                    x = src[rows, lanes(i)] if j == 0 else xs[w, j - 1, rows, lanes(i)]
                    sums[j] = g0 * x if sums[j] is None else sums[j] + g0 * x
            for j in range(SHORT):
                acc[lax.rem(t, 2), w * 3 + j, own_rows, :] = sums[j]
            heads[lax.rem(t, 2), w, own_rows, :] = gw[w][0]

    halves = ((iota((8, 2 * LANE), 1) // LANE) == iota((8, 2 * LANE), 0)).astype(F32).astype(BF)

    def lane_sums(a, b, c, d):
        sums = nt(
            halves,
            jnp.concatenate(
                [jnp.concatenate([a, b], axis=1), jnp.concatenate([c, d], axis=1)], axis=0
            ),
        )
        return [sums[0:1, :LANE], sums[1:2, :LANE], sums[0:1, LANE:], sums[1:2, LANE:]]

    def tile_sums(t):
        cols = pl.ds(pl.multiple_of(t * TILE, TILE), TILE)
        k = lax.rem(t, 2)
        edge = (
            nt(pick(0, 0), heads[k, 0]) + nt(pick(1, 0), heads[k, 1]) + nt(pick(2, 0), heads[k, 2])
        )
        edge_s[:, cols] = edge
        rim = rim_r[:, cols]
        sums = lane_sums(acc[k, 0], acc[k, 1], acc[k, 2], acc[k, 3])
        sums += lane_sums(acc[k, 4], acc[k, 5], acc[k, 6], acc[k, 7])
        sums += lane_sums(acc[k, 8], acc[k, 9], acc[k, 8], acc[k, 9])
        blank = jnp.zeros((2, LANE), F32)
        for w in range(3):
            g0, g1 = edge[2 * w : 2 * w + 1], edge[2 * w + 1 : 2 * w + 2]
            x2, x1 = rim[2 * w : 2 * w + 1], rim[2 * w + 1 : 2 * w + 2]
            row1 = sums[w * 3 + 1] + g0 * x1
            row2 = sums[w * 3 + 2] + g0 * x2 + g1 * x1
            msg_s[t * 4 + w, 2:8, :] = jnp.concatenate([sums[9], sums[w * 3], row1, row2, blank], axis=0)
        msg_s[t * 4 + 3, 2:8, :] = jnp.concatenate([sums[9], blank, blank, blank[:1]], axis=0)

    def send_sums(t):
        for i in range(4):
            o = t * 4 + i

            @pl.when(o != me)
            def _():
                msg_copy(o).start()

    def main_tile(step, before, ahead):
        t = tile_at(step)
        if ahead:
            halo_ready(tile_at(step + 1) * TILE)
        groups = TILE // GROUP
        matmuls(t, 0)
        if before:
            tile_sums(tile_at(step - 1))
        for u in range(groups):
            gradients(t, u)
            if u + 1 < groups:
                matmuls(t, u + 1)
            if ahead and u == 2:
                rims_in(tile_at(step + 1))
        if before:
            send_sums(tile_at(step - 1))

    def tile_at(step):
        return (step + tiles // 2) % tiles

    def middle_tile(step, carry):
        main_tile(step, True, True)
        return carry

    halo_ready(tile_at(0) * TILE)
    rims_in(tile_at(0))
    main_tile(0, False, True)
    lax.fori_loop(1, tiles - 1, middle_tile, 0)
    main_tile(tiles - 1, True, False)
    tile_sums(tile_at(tiles - 1))
    send_sums(tile_at(tiles - 1))

    edge_copy = pltpu.make_async_remote_copy(
        src_ref=edge_s, dst_ref=edge_r, send_sem=edge_sem.at[0], recv_sem=edge_sem.at[1],
        device_id={"ctx": left}, device_id_type=MESH,
    )

    @pl.when(has_left)
    def _():
        edge_copy.start()

    def output_rows(t):
        for u in range(4):
            rows = pl.ds(pl.multiple_of(t * 64 + u * GROUP, GROUP), GROUP)
            for w, dst in enumerate((out_q, out_k, out_v)):
                tap = tap_of(w, rows)
                a1 = a2 = None
                for i in reversed(range(blocks)):
                    g0 = raw[w, rows, lanes(i)]
                    r1, r2 = pltpu.roll(g0, LANE - 1, 1), pltpu.roll(g0, LANE - 2, 1)
                    dst[rows, lanes(i)] = (
                        tap[0] * g0 + tap[1] * shift_left(r1, a1, last1) + tap[2] * shift_left(r2, a2, last2)
                    )
                    a1, a2 = r1, r2

    def output_loop(t, carry):
        output_rows(t)
        return carry

    early_rows = 2 * tiles - tiles // 2
    lax.fori_loop(0, early_rows, output_loop, 0)

    msg_r[me] = msg_s[me]
    drain(msg_r.at[others], msg_sem.at[1])

    total = msg_r[0]
    for o in range(1, n):
        total = total + msg_r[o]
    tot_s[...] = jnp.concatenate([total[3:6], jnp.zeros((5, LANE), F32)], axis=0)

    def tot_copy(k):
        return pltpu.make_async_remote_copy(
            src_ref=tot_s, dst_ref=tot_r.at[me], send_sem=tot_sem.at[0], recv_sem=tot_sem.at[1],
            device_id={"ctx": peer(k)}, device_id_type=MESH,
        )

    for k in range(n - 1):
        tot_copy(k).start()

    lax.fori_loop(early_rows, 2 * tiles, output_loop, 0)
    tot_r[me] = tot_s[...]
    out_filt[...] = lax.dot_general(
        total, flip.astype(F32), (((1,), (0,)), ((), ())),
        preferred_element_type=F32, precision=lax.Precision.HIGHEST,
    )[0:2]
    out_bias[...] = pltpu.roll(total[2:3], lax.rem(LANE - lax.rem(me, 4) * 32, LANE), 1)

    @pl.when(has_right)
    def _():
        edge_copy.wait_recv()

    out_edge[...] = edge_r[...]

    drain(filt_r.at[others], filt_sem.at[0])
    drain(msg_r.at[others], msg_sem.at[0])

    @pl.when(has_right)
    def _():
        rim_copy.wait_send()
        for c in range(chunks):
            ph_copy(c).wait_send()

    @pl.when(has_left)
    def _():
        col_copy.wait_send()
        edge_copy.wait_send()
        for c in range(chunks):
            gh_copy(c).wait_send()

    drain(tot_r.at[others], tot_sem.at[1])
    for w in range(3):
        for t in range(tiles):
            out_short[w, :, t * TILE : (t + 1) * TILE] = tot_r[t * 4 + w, 0:SHORT, :]
    drain(tot_r.at[others], tot_sem.at[0])


def finish(
    blocks,
    gq, gk, gv, edge, short, filt, bias, taps_hbm,
    out_q, out_k, out_v, out_short, out_filt, out_bias,
    taps, ends, bias_v, sem, end_sem,
):
    last = blocks - 1
    bulk = pl.ds(0, last * LANE)
    copies = [pltpu.make_async_copy(taps_hbm, taps, sem.at[0])]
    for i, (src, dst) in enumerate(((gq, out_q), (gk, out_k), (gv, out_v))):
        copies.append(pltpu.make_async_copy(src.at[:, bulk], dst.at[:, bulk], sem.at[1 + i]))
    copies.append(pltpu.make_async_copy(short, out_short, sem.at[4]))
    copies.append(pltpu.make_async_copy(filt, out_filt, sem.at[5]))
    for copy in copies:
        copy.start()
    bias_v[...] = bias[0, : bias_v.shape[0]]
    copies.append(pltpu.make_async_copy(bias_v, out_bias, sem.at[6]))
    copies[-1].start()
    copies[0].wait()
    rim_place = place((LANE - 2, LANE - 2, LANE - 2))
    for t in range(gq.shape[0] // TILE):
        cols = pl.ds(t * TILE, TILE)
        x = edge[:, cols]
        rows = []
        for w in range(3):
            tap1, tap2 = taps[w, 1:2, cols], taps[w, 2:3, cols]
            g0, g1 = x[2 * w : 2 * w + 1], x[2 * w + 1 : 2 * w + 2]
            rows += [tap2 * g0, tap1 * g0 + tap2 * g1]
        rows.append(jnp.zeros((10, TILE), F32))
        fix = tn(jnp.concatenate(rows, axis=0).astype(BF), rim_place).astype(BF)
        for w, src in enumerate((gq, gk, gv)):
            ends[w, cols, :] = src[cols, lanes(last)] + fix[:, w * LANE : (w + 1) * LANE]
    for w, dst in enumerate((out_q, out_k, out_v)):
        copies.append(pltpu.make_async_copy(ends.at[w], dst.at[:, lanes(last)], end_sem.at[w]))
        copies[-1].start()
    for copy in copies[1:]:
        copy.wait()


def body(query_feat, key_feat, value_feat, grad_out, short_taps, filters, skip_bias):
    channels, length = query_feat.shape
    n = lax.axis_size("ctx")
    blocks = length // LANE
    full, tile = (channels, length), (channels, LANE)
    vmem = pl.BlockSpec(memory_space=pltpu.VMEM)
    hbm = pl.BlockSpec(memory_space=pltpu.HBM)
    dma = pltpu.SemaphoreType.DMA
    row = pltpu.VMEM((8, channels), F32)
    slots = pltpu.VMEM((n, 8, LANE), F32)
    one = pltpu.VMEM((8, LANE), F32)
    short_taps, filters, skip_bias = [
        pltpu.with_memory_space_constraint(x, pltpu.HBM) for x in (short_taps, filters, skip_bias)
    ]
    outs = pl.pallas_call(
        functools.partial(kernel, n, blocks),
        out_shape=(
            pltpu.VMEM(full, BF), pltpu.VMEM(full, BF), pltpu.VMEM(full, BF),
            row,
            pltpu.VMEM(short_taps.shape, F32),
            pltpu.VMEM(filters.shape, F32),
            pltpu.VMEM((1, LANE), F32),
        ),
        in_specs=[hbm] * 7,
        out_specs=(vmem,) * 7,
        scratch_shapes=[pltpu.VMEM(full, BF)] * 9
        + [
            pltpu.VMEM((3, channels, length), BF),
            pltpu.VMEM((3, 2, channels, length), BF),
            pltpu.VMEM((2, 2, blocks * GROUP, LANE), BF),
            pltpu.VMEM((2, 10, TILE, LANE), BF),
            pltpu.VMEM((2, 3, TILE, LANE), BF),
            pltpu.VMEM(tile, BF), pltpu.VMEM(tile, BF),
            pltpu.VMEM(tile, BF), pltpu.VMEM(tile, BF),
            pltpu.VMEM(short_taps.shape, F32),
            pltpu.VMEM(filters.shape, BF),
            pltpu.VMEM(skip_bias.shape, BF),
            pltpu.VMEM((9, channels, LANE), BF),
            pltpu.VMEM(tile, BF),
            row, row, row, row, one, slots, slots, slots, one, slots, row, row,
            dma((12,)), dma((2,)), dma((2,)),
            dma((CHUNKS,)), dma((CHUNKS,)), dma((CHUNKS,)), dma((CHUNKS,)),
            dma((2,)), dma((2,)), dma((2,)), dma((2,)),
        ],
        compiler_params=pltpu.CompilerParams(
            collective_id=0, has_side_effects=True, vmem_limit_bytes=48 * 1024 * 1024
        ),
    )(query_feat, key_feat, value_feat, grad_out, short_taps, filters, skip_bias)
    return pl.pallas_call(
        functools.partial(finish, blocks),
        out_shape=tuple(
            jax.ShapeDtypeStruct(s, d)
            for s, d in (
                (full, BF), (full, BF), (full, BF),
                (short_taps.shape, F32), (filters.shape, F32), (skip_bias.shape, F32),
            )
        ),
        in_specs=[vmem] * 7 + [hbm],
        out_specs=(hbm,) * 6,
        scratch_shapes=[
            pltpu.VMEM(short_taps.shape, F32),
            pltpu.VMEM((3,) + tile, BF),
            pltpu.VMEM(skip_bias.shape, F32),
            dma((7,)), dma((3,)),
        ],
        compiler_params=pltpu.CompilerParams(vmem_limit_bytes=16 * 1024 * 1024),
    )(*outs, short_taps)


def solution(mesh):
    wide, narrow = P("tp", "ctx"), P(None, None, "tp")
    both = ("tp", "ctx")

    def whole(*args):
        with jax.sharding.use_abstract_mesh(mesh.abstract_mesh):
            return jax.shard_map(
                body,
                mesh=mesh,
                in_specs=(wide, wide, wide, wide, narrow, P(both, None), P(both)),
                out_specs=(wide, wide, wide, narrow, P(both, None), P(both)),
                check_vma=False,
            )(*args)

    return whole
```

```python
import functools

import jax
import jax.numpy as jnp
from jax import lax
from jax.experimental import pallas as pl
from jax.experimental.pallas import tpu as pltpu
from jax.sharding import PartitionSpec as P

TAPS = 128
SHORT = 3
GROUP = 16
LANE = 128
TILE = 128
CHUNKS = 4
BF = jnp.bfloat16
F32 = jnp.float32
MESH = pl.DeviceIdType.MESH


def nn(a, b):
    return lax.dot_general(a, b, (((1,), (0,)), ((), ())), preferred_element_type=F32)


def nt(a, b):
    return lax.dot_general(a, b, (((1,), (1,)), ((), ())), preferred_element_type=F32)


def tn(a, b):
    return lax.dot_general(a, b, (((0,), (0,)), ((), ())), preferred_element_type=F32)


def iota(shape, axis):
    return lax.broadcasted_iota(jnp.int32, shape, axis)


def lanes(i):
    return pl.ds(i * LANE, LANE)


def place(firsts):
    sub, lane = iota((16, LANE), 0), iota((16, LANE), 1)
    blocks = [
        ((sub // 2 == w) & (lane == first + sub % 2)).astype(F32).astype(BF)
        for w, first in enumerate(firsts)
    ]
    return jnp.concatenate(blocks, axis=1)


def kernel(
    n, blocks,
    q_hbm, k_hbm, v_hbm, g_hbm, taps_hbm, filt_hbm, bias_hbm,
    out_q, out_k, out_v, out_edge, out_short, out_filt, out_bias,
    qx, kx, vx, gx, kc, vc, pr, gm, gmr, raw, xs, conv, acc, heads, first, after, ph, gh, taps, filt_in, bias_in, taps_b, bias_b,
    rim_s, rim_r, col_s, col_r, filt_s, filt_r, msg_s, msg_r, tot_s, tot_r, edge_s, edge_r,
    in_sem, rim_sem, col_sem, ph_ssem, ph_rsem, gh_ssem, gh_rsem, filt_sem, msg_sem, tot_sem, edge_sem,
):
    me = lax.axis_index("ctx")
    channels = qx.shape[0]
    tiles = channels // TILE
    chunks = min(CHUNKS, tiles)
    last = blocks - 1
    part = channels // chunks
    right, left = lax.rem(me + 1, n), lax.rem(me + n - 1, n)
    has_left, has_right = me > 0, me < n - 1

    def peer(k):
        if n != 32:
            return lax.rem(me + 1 + k, n)
        i, j = k // 8, k // 2 % 4
        dz = 1 + 2 * i - 3 * (i // 2)
        dx = 2 - j + 3 * (j // 2) + 2 * (j // 3)
        z, x, c = (me // 8 + dz) % 4, (me // 2 + dx) % 4, (me + 1 + k % 2) % 2
        return z * 8 + x * 2 + c

    barrier = pltpu.get_barrier_semaphore()
    for k in range(n - 1):
        pl.semaphore_signal(barrier, inc=1, device_id={"ctx": peer(k)}, device_id_type=MESH)

    def piece(i, src, dst, start, size):
        cols = pl.ds(start * LANE, size * LANE)
        return pltpu.make_async_copy(src.at[:, cols], dst.at[:, cols], in_sem.at[i])

    loads = [
        pltpu.make_async_copy(taps_hbm, taps, in_sem.at[0]),
        pltpu.make_async_copy(filt_hbm, filt_in, in_sem.at[1]),
        pltpu.make_async_copy(bias_hbm, bias_in, in_sem.at[2]),
        piece(3, k_hbm, kx, blocks - 2, 2),
        piece(4, v_hbm, vx, blocks - 2, 2),
        piece(5, q_hbm, qx, last, 1),
        piece(6, q_hbm, qx, 0, 1),
        piece(7, g_hbm, gx, 0, 1),
        piece(8, k_hbm, kx, 0, blocks - 2),
        piece(9, v_hbm, vx, 0, blocks - 2),
        piece(10, q_hbm, qx, 1, blocks - 2),
        piece(11, g_hbm, gx, 1, blocks - 1),
    ]
    for load in loads:
        load.start()

    lane16 = iota((GROUP, LANE), 1)
    first1, first2 = lane16 < 1, lane16 < 2
    last1, last2 = lane16 >= LANE - 1, lane16 >= LANE - 2
    zero16 = jnp.zeros((GROUP, LANE), BF)
    eye = iota((TILE, TILE), 0) == iota((TILE, TILE), 1)
    ones = jnp.ones((TILE, LANE), BF)
    flip = (iota((LANE, LANE), 0) + iota((LANE, LANE), 1) == LANE - 1).astype(F32).astype(BF)

    def spread(row):
        return nn(jnp.where(eye, row, 0.0).astype(BF), ones).astype(BF)

    def tap_tile(t):
        cols = pl.ds(pl.multiple_of(t * TILE, TILE), TILE)
        for w in range(3):
            for j in range(SHORT):
                taps_b[w * 3 + j, cols, :] = spread(taps[w, j : j + 1, cols])

    loads[0].wait()
    tap_tile(0)

    loads[1].wait()
    loads[2].wait()
    own_bias = bias_in[...].astype(F32).reshape(1, -1)
    own_bias = jnp.pad(own_bias, ((0, 0), (0, LANE - own_bias.shape[1])))
    own_bias = pltpu.roll(own_bias, lax.rem(me, 4) * 32, 1)
    filt_s[...] = jnp.concatenate(
        [filt_in[...].astype(F32), own_bias, jnp.zeros((5, LANE), F32)], axis=0
    )
    filt_r[me] = filt_s[...]

    sub8, lane8 = iota((8, LANE), 0), iota((8, LANE), 1)

    def pick(w, first_lane):
        return ((sub8 // 2 == w) & (lane8 == first_lane + sub8 % 2)).astype(F32).astype(BF)

    def shift_right(cur, before, mask):
        return jnp.where(mask, zero16 if before is None else before, cur)

    def short_forward(w, rows, i, tap, x, r1, r2, b1, b2):
        s1, s2 = shift_right(r1, b1, first1), shift_right(r2, b2, first2)
        xs[w, 0, rows, lanes(i)] = s1
        xs[w, 1, rows, lanes(i)] = s2
        return tap[0] * x + tap[1] * s1 + tap[2] * s2

    for load in loads[3:8]:
        load.wait()
    rim_s[...] = (
        nt(pick(0, LANE - 2), qx[:, lanes(last)])
        + nt(pick(1, LANE - 2), kx[:, lanes(last)])
        + nt(pick(2, LANE - 2), vx[:, lanes(last)])
    )
    col_s[...] = nt(pick(0, 0), gx[:, lanes(0)])

    def tap_of(w, rows):
        return [taps_b[w * 3 + j, rows, :] for j in range(SHORT)]

    def border_tile(t):
        for u in range(TILE // GROUP):
            rows = pl.ds(pl.multiple_of(t * TILE + u * GROUP, GROUP), GROUP)
            kv = []
            for w, (src, dst) in ((1, (kx, kc)), (2, (vx, vc))):
                x, prev = src[rows, lanes(last)], src[rows, lanes(last - 1)]
                y = short_forward(
                    w, rows, last, tap_of(w, rows), x, pltpu.roll(x, 1, 1), pltpu.roll(x, 2, 1),
                    pltpu.roll(prev, 1, 1), pltpu.roll(prev, 2, 1),
                )
                dst[rows, lanes(last)] = y
                kv.append(y)
            pr[rows, lanes(last)] = kv[0] * kv[1]
            x = qx[rows, lanes(0)]
            y = short_forward(
                0, rows, 0, tap_of(0, rows), x, pltpu.roll(x, 1, 1), pltpu.roll(x, 2, 1), None, None
            )
            gm[rows, lanes(0)] = gx[rows, lanes(0)] * y

    def start_tile(t, carry):
        tap_tile(t)
        border_tile(t - 1)
        return carry

    lax.fori_loop(1, tiles, start_tile, 0)
    border_tile(tiles - 1)

    pl.semaphore_wait(barrier, n - 1)

    rim_copy = pltpu.make_async_remote_copy(
        src_ref=rim_s, dst_ref=rim_r, send_sem=rim_sem.at[0], recv_sem=rim_sem.at[1],
        device_id={"ctx": right}, device_id_type=MESH,
    )
    col_copy = pltpu.make_async_remote_copy(
        src_ref=col_s, dst_ref=col_r, send_sem=col_sem.at[0], recv_sem=col_sem.at[1],
        device_id={"ctx": left}, device_id_type=MESH,
    )

    def ph_copy(c):
        rows = pl.ds(c * part, part)
        return pltpu.make_async_remote_copy(
            src_ref=pr.at[rows, lanes(last)], dst_ref=ph.at[rows, :],
            send_sem=ph_ssem.at[c], recv_sem=ph_rsem.at[c],
            device_id={"ctx": right}, device_id_type=MESH,
        )

    def gh_copy(c):
        rows = pl.ds(c * part, part)
        return pltpu.make_async_remote_copy(
            src_ref=gm.at[rows, lanes(0)], dst_ref=gh.at[rows, :],
            send_sem=gh_ssem.at[c], recv_sem=gh_rsem.at[c],
            device_id={"ctx": left}, device_id_type=MESH,
        )

    def filt_copy(k):
        return pltpu.make_async_remote_copy(
            src_ref=filt_s, dst_ref=filt_r.at[me], send_sem=filt_sem.at[0], recv_sem=filt_sem.at[1],
            device_id={"ctx": peer(k)}, device_id_type=MESH,
        )

    for k in range(n - 1):
        filt_copy(k).start()

    order = [(c + chunks // 2) % chunks for c in range(chunks)]

    @pl.when(has_right)
    def _():
        rim_copy.start()
        for c in order:
            ph_copy(c).start()

    @pl.when(has_left)
    def _():
        col_copy.start()
        for c in order:
            gh_copy(c).start()

    for load in loads[8:]:
        load.wait()

    def forward_rows(t, carry):
        turned = []
        for u in range(8):
            rows = pl.ds(pl.multiple_of(t * 128 + u * GROUP, GROUP), GROUP)
            taps3 = [tap_of(w, rows) for w in range(3)]
            b1, b2 = [None] * 3, [None] * 3
            for i in range(blocks):
                short = [None] * 3
                for w, src in enumerate((qx, kx, vx)):
                    if i == last and w > 0:
                        continue
                    x = src[rows, lanes(i)]
                    r1, r2 = pltpu.roll(x, 1, 1), pltpu.roll(x, 2, 1)
                    if i > 0 or w > 0:
                        short[w] = short_forward(w, rows, i, taps3[w], x, r1, r2, b1[w], b2[w])
                    b1[w], b2[w] = r1, r2
                if i < last:
                    kc[rows, lanes(i)] = short[1]
                    vc[rows, lanes(i)] = short[2]
                    pr[rows, lanes(i)] = short[1] * short[2]
                if i > 0:
                    m = gx[rows, lanes(i)] * short[0]
                    gm[rows, lanes(i)] = m
                    turned.append(m)
        turned = nn(jnp.concatenate(turned, axis=0), flip).astype(BF)
        for u in range(8):
            rows = pl.ds(pl.multiple_of(t * 128 + u * GROUP, GROUP), GROUP)
            for i in range(1, blocks):
                at = (u * last + i - 1) * GROUP
                gmr[rows, lanes(i)] = turned[at : at + GROUP]
        return carry

    lax.fori_loop(0, channels // 128, forward_rows, 0)

    @pl.when(has_left)
    def _():
        rim_copy.wait_recv()

    @pl.when(jnp.logical_not(has_left))
    def _():
        rim_r[...] = jnp.zeros(rim_r.shape, F32)
        ph[...] = jnp.zeros(ph.shape, BF)

    @pl.when(has_right)
    def _():
        col_copy.wait_recv()

    @pl.when(jnp.logical_not(has_right))
    def _():
        col_r[...] = jnp.zeros(col_r.shape, F32)
        edge_r[...] = jnp.zeros(edge_r.shape, F32)
        gh[...] = jnp.zeros(gh.shape, BF)

    def drain(ref, sem):
        pltpu.make_async_copy(ref, ref, sem).wait()

    others = pl.ds(0, n - 1)
    drain(filt_r.at[others], filt_sem.at[1])

    sq_row, sq_col = iota((LANE, LANE), 0), iota((LANE, LANE), 1)
    upper = sq_col >= sq_row
    early = sq_col + sq_row <= LANE - 1
    zero_sq = jnp.zeros((LANE, LANE), BF)
    rim_place = place((0, 0, 0, 0))
    pad = jnp.zeros((GROUP, LANE), BF)

    def shift_left(cur, after, mask):
        return jnp.where(mask, zero16 if after is None else after, cur)

    def msg_copy(o):
        return pltpu.make_async_remote_copy(
            src_ref=msg_s.at[o], dst_ref=msg_r.at[me], send_sem=msg_sem.at[0], recv_sem=msg_sem.at[1],
            device_id={"ctx": o}, device_id_type=MESH,
        )

    def halo_ready(base):
        for c in range(chunks):
            @pl.when(base == c * part)
            def _():
                @pl.when(has_left)
                def _():
                    ph_copy(c).wait_recv()

                @pl.when(has_right)
                def _():
                    gh_copy(c).wait_recv()

    def rims_in(t):
        cols = pl.ds(pl.multiple_of(t * TILE, TILE), TILE)
        rim, own, far = rim_r[:, cols], rim_s[:, cols], col_r[:, cols]
        rows = []
        for w in range(3):
            tap1, tap2 = taps[w, 1:2, cols], taps[w, 2:3, cols]
            x2, x1 = rim[2 * w : 2 * w + 1], rim[2 * w + 1 : 2 * w + 2]
            rows += [tap1 * x1 + tap2 * x2, tap2 * x1]
        tap1, tap2 = taps[0, 1:2, cols], taps[0, 2:3, cols]
        rows += [far[0:1] * (tap1 * own[1:2] + tap2 * own[0:1]), far[1:2] * (tap2 * own[1:2])]
        rows.append(jnp.zeros((8, TILE), F32))
        fix = tn(jnp.concatenate(rows, axis=0).astype(BF), rim_place).astype(BF)
        kk = kc[cols, lanes(0)] + fix[:, LANE : 2 * LANE]
        vv = vc[cols, lanes(0)] + fix[:, 2 * LANE : 3 * LANE]
        kc[cols, lanes(0)] = kk
        vc[cols, lanes(0)] = vv
        pr[cols, lanes(0)] = kk * vv
        m0 = gm[cols, lanes(0)] + gx[cols, lanes(0)] * fix[:, :LANE]
        first[cols, :] = m0
        gmr[cols, lanes(0)] = nn(m0, flip).astype(BF)
        after[cols, :] = gh[cols, :] + fix[:, 3 * LANE :]
        bias_b[cols, :] = spread(
            filt_r[t * 4, 2:3, :] + filt_r[t * 4 + 1, 2:3, :]
            + filt_r[t * 4 + 2, 2:3, :] + filt_r[t * 4 + 3, 2:3, :]
        )

    depth = blocks * GROUP

    def matmuls(t, u):
        rows = pl.ds(pl.multiple_of(t * TILE + u * GROUP, GROUP), GROUP)
        slot = t * 4 + u // 2
        filt = filt_r[slot, u % 2 : u % 2 + 1, :].astype(BF)
        round_filt = pltpu.roll(jnp.broadcast_to(filt, (LANE, LANE)), 0, 1, stride=1, stride_axis=0)
        now = jnp.where(upper, round_filt, zero_sq)
        then = jnp.where(upper, zero_sq, round_filt)
        p = [ph[rows, :]] + [pr[rows, lanes(i)] for i in range(blocks)]
        m = [first[rows, :]] + [gm[rows, lanes(i)] for i in range(1, blocks)] + [after[rows, :]]
        p_ext = jnp.concatenate(p, axis=0)
        m_ext = jnp.concatenate(m, axis=0)
        conv[u % 2, 0] = nn(
            jnp.concatenate([p_ext[:depth], p_ext[GROUP:]], axis=1),
            jnp.concatenate([then, now], axis=0),
        ).astype(BF)
        conv[u % 2, 1] = nt(
            jnp.concatenate([m_ext[:depth], m_ext[GROUP:]], axis=1),
            jnp.concatenate([now, then], axis=1),
        ).astype(BF)
        m_rev = [gmr[rows, lanes(i)] for i in range(blocks)]
        diff = tn(
            p_ext,
            jnp.concatenate(
                [jnp.concatenate(m_rev + [pad], axis=0), jnp.concatenate([pad] + m_rev, axis=0)], axis=1
            ),
        )
        diff = jnp.where(early, diff[:, LANE:], diff[:, :LANE]).astype(BF)
        diff = pltpu.roll(diff, 0, 1, stride=1, stride_axis=0)
        msg_s[slot, u % 2 : u % 2 + 1, :] = jnp.sum(diff.astype(F32), axis=0, keepdims=True)

    def gradients(t, u):
        rows = pl.ds(pl.multiple_of(t * TILE + u * GROUP, GROUP), GROUP)
        own_rows = pl.ds(u * GROUP, GROUP)
        bias = bias_b[rows, :]
        bias_sum = None
        gw = [[None] * blocks for _ in range(3)]
        for i in range(blocks):
            p = pr[rows, lanes(i)]
            m = first[rows, :] if i == 0 else gm[rows, lanes(i)]
            mixed = conv[u % 2, 0, pl.ds(i * GROUP, GROUP), :] + bias * p
            back = conv[u % 2, 1, pl.ds(i * GROUP, GROUP), :] + bias * m
            gw[0][i] = gx[rows, lanes(i)] * mixed
            gw[1][i] = back * vc[rows, lanes(i)]
            gw[2][i] = back * kc[rows, lanes(i)]
            term = m * p
            bias_sum = term if bias_sum is None else bias_sum + term
        acc[lax.rem(t, 2), 9, own_rows, :] = bias_sum
        for w, src in enumerate((qx, kx, vx)):
            sums = [None] * SHORT
            for i in range(blocks):
                g0 = gw[w][i]
                raw[w, rows, lanes(i)] = g0
                for j in range(SHORT):
                    x = src[rows, lanes(i)] if j == 0 else xs[w, j - 1, rows, lanes(i)]
                    sums[j] = g0 * x if sums[j] is None else sums[j] + g0 * x
            for j in range(SHORT):
                acc[lax.rem(t, 2), w * 3 + j, own_rows, :] = sums[j]
            heads[lax.rem(t, 2), w, own_rows, :] = gw[w][0]

    halves = ((iota((8, 2 * LANE), 1) // LANE) == iota((8, 2 * LANE), 0)).astype(F32).astype(BF)

    def lane_sums(a, b, c, d):
        sums = nt(
            halves,
            jnp.concatenate(
                [jnp.concatenate([a, b], axis=1), jnp.concatenate([c, d], axis=1)], axis=0
            ),
        )
        return [sums[0:1, :LANE], sums[1:2, :LANE], sums[0:1, LANE:], sums[1:2, LANE:]]

    def tile_sums(t):
        cols = pl.ds(pl.multiple_of(t * TILE, TILE), TILE)
        k = lax.rem(t, 2)
        edge = (
            nt(pick(0, 0), heads[k, 0]) + nt(pick(1, 0), heads[k, 1]) + nt(pick(2, 0), heads[k, 2])
        )
        edge_s[:, cols] = edge
        rim = rim_r[:, cols]
        sums = lane_sums(acc[k, 0], acc[k, 1], acc[k, 2], acc[k, 3])
        sums += lane_sums(acc[k, 4], acc[k, 5], acc[k, 6], acc[k, 7])
        sums += lane_sums(acc[k, 8], acc[k, 9], acc[k, 8], acc[k, 9])
        blank = jnp.zeros((2, LANE), F32)
        for w in range(3):
            g0, g1 = edge[2 * w : 2 * w + 1], edge[2 * w + 1 : 2 * w + 2]
            x2, x1 = rim[2 * w : 2 * w + 1], rim[2 * w + 1 : 2 * w + 2]
            row1 = sums[w * 3 + 1] + g0 * x1
            row2 = sums[w * 3 + 2] + g0 * x2 + g1 * x1
            msg_s[t * 4 + w, 2:8, :] = jnp.concatenate([sums[9], sums[w * 3], row1, row2, blank], axis=0)
        msg_s[t * 4 + 3, 2:8, :] = jnp.concatenate([sums[9], blank, blank, blank[:1]], axis=0)

    def send_sums(t):
        for i in range(4):
            o = t * 4 + i

            @pl.when(o != me)
            def _():
                msg_copy(o).start()

    def main_tile(step, before, ahead):
        t = tile_at(step)
        if ahead:
            halo_ready(tile_at(step + 1) * TILE)
        groups = TILE // GROUP
        matmuls(t, 0)
        if before:
            tile_sums(tile_at(step - 1))
        for u in range(groups):
            gradients(t, u)
            if u + 1 < groups:
                matmuls(t, u + 1)
            if ahead and u == 2:
                rims_in(tile_at(step + 1))
        if before:
            send_sums(tile_at(step - 1))

    def tile_at(step):
        return (step + tiles // 2) % tiles

    def middle_tile(step, carry):
        main_tile(step, True, True)
        return carry

    halo_ready(tile_at(0) * TILE)
    rims_in(tile_at(0))
    main_tile(0, False, True)
    lax.fori_loop(1, tiles - 1, middle_tile, 0)
    main_tile(tiles - 1, True, False)
    tile_sums(tile_at(tiles - 1))
    send_sums(tile_at(tiles - 1))

    edge_copy = pltpu.make_async_remote_copy(
        src_ref=edge_s, dst_ref=edge_r, send_sem=edge_sem.at[0], recv_sem=edge_sem.at[1],
        device_id={"ctx": left}, device_id_type=MESH,
    )

    @pl.when(has_left)
    def _():
        edge_copy.start()

    def output_rows(t):
        for u in range(4):
            rows = pl.ds(pl.multiple_of(t * 64 + u * GROUP, GROUP), GROUP)
            for w, dst in enumerate((out_q, out_k, out_v)):
                tap = tap_of(w, rows)
                a1 = a2 = None
                for i in reversed(range(blocks)):
                    g0 = raw[w, rows, lanes(i)]
                    r1, r2 = pltpu.roll(g0, LANE - 1, 1), pltpu.roll(g0, LANE - 2, 1)
                    dst[rows, lanes(i)] = (
                        tap[0] * g0 + tap[1] * shift_left(r1, a1, last1) + tap[2] * shift_left(r2, a2, last2)
                    )
                    a1, a2 = r1, r2

    def output_loop(t, carry):
        output_rows(t)
        return carry

    early_rows = 2 * tiles - tiles // 2
    lax.fori_loop(0, early_rows, output_loop, 0)

    msg_r[me] = msg_s[me]
    drain(msg_r.at[others], msg_sem.at[1])

    total = msg_r[0]
    for o in range(1, n):
        total = total + msg_r[o]
    tot_s[...] = jnp.concatenate([total[3:6], jnp.zeros((5, LANE), F32)], axis=0)

    def tot_copy(k):
        return pltpu.make_async_remote_copy(
            src_ref=tot_s, dst_ref=tot_r.at[me], send_sem=tot_sem.at[0], recv_sem=tot_sem.at[1],
            device_id={"ctx": peer(k)}, device_id_type=MESH,
        )

    for k in range(n - 1):
        tot_copy(k).start()

    lax.fori_loop(early_rows, 2 * tiles, output_loop, 0)
    tot_r[me] = tot_s[...]
    out_filt[...] = lax.dot_general(
        total, flip.astype(F32), (((1,), (0,)), ((), ())),
        preferred_element_type=F32, precision=lax.Precision.HIGHEST,
    )[0:2]
    out_bias[...] = pltpu.roll(total[2:3], lax.rem(LANE - lax.rem(me, 4) * 32, LANE), 1)

    @pl.when(has_right)
    def _():
        edge_copy.wait_recv()

    out_edge[...] = edge_r[...]

    drain(filt_r.at[others], filt_sem.at[0])
    drain(msg_r.at[others], msg_sem.at[0])

    @pl.when(has_right)
    def _():
        rim_copy.wait_send()
        for c in range(chunks):
            ph_copy(c).wait_send()

    @pl.when(has_left)
    def _():
        col_copy.wait_send()
        edge_copy.wait_send()
        for c in range(chunks):
            gh_copy(c).wait_send()

    drain(tot_r.at[others], tot_sem.at[1])
    for w in range(3):
        for t in range(tiles):
            out_short[w, :, t * TILE : (t + 1) * TILE] = tot_r[t * 4 + w, 0:SHORT, :]
    drain(tot_r.at[others], tot_sem.at[0])


def finish(
    blocks,
    gq, gk, gv, edge, short, filt, bias, taps_hbm,
    out_q, out_k, out_v, out_short, out_filt, out_bias,
    taps, ends, bias_v, sem, end_sem,
):
    last = blocks - 1
    bulk = pl.ds(0, last * LANE)
    copies = [pltpu.make_async_copy(taps_hbm, taps, sem.at[0])]
    for i, (src, dst) in enumerate(((gq, out_q), (gk, out_k), (gv, out_v))):
        copies.append(pltpu.make_async_copy(src.at[:, bulk], dst.at[:, bulk], sem.at[1 + i]))
    copies.append(pltpu.make_async_copy(short, out_short, sem.at[4]))
    copies.append(pltpu.make_async_copy(filt, out_filt, sem.at[5]))
    for copy in copies:
        copy.start()
    bias_v[...] = bias[0, : bias_v.shape[0]]
    copies.append(pltpu.make_async_copy(bias_v, out_bias, sem.at[6]))
    copies[-1].start()
    copies[0].wait()
    rim_place = place((LANE - 2, LANE - 2, LANE - 2))
    for t in range(gq.shape[0] // TILE):
        cols = pl.ds(t * TILE, TILE)
        x = edge[:, cols]
        rows = []
        for w in range(3):
            tap1, tap2 = taps[w, 1:2, cols], taps[w, 2:3, cols]
            g0, g1 = x[2 * w : 2 * w + 1], x[2 * w + 1 : 2 * w + 2]
            rows += [tap2 * g0, tap1 * g0 + tap2 * g1]
        rows.append(jnp.zeros((10, TILE), F32))
        fix = tn(jnp.concatenate(rows, axis=0).astype(BF), rim_place).astype(BF)
        for w, src in enumerate((gq, gk, gv)):
            ends[w, cols, :] = src[cols, lanes(last)] + fix[:, w * LANE : (w + 1) * LANE]
    for w, dst in enumerate((out_q, out_k, out_v)):
        copies.append(pltpu.make_async_copy(ends.at[w], dst.at[:, lanes(last)], end_sem.at[w]))
        copies[-1].start()
    for copy in copies[1:]:
        copy.wait()


def body(query_feat, key_feat, value_feat, grad_out, short_taps, filters, skip_bias):
    channels, length = query_feat.shape
    n = lax.axis_size("ctx")
    blocks = length // LANE
    full, tile = (channels, length), (channels, LANE)
    vmem = pl.BlockSpec(memory_space=pltpu.VMEM)
    hbm = pl.BlockSpec(memory_space=pltpu.HBM)
    dma = pltpu.SemaphoreType.DMA
    row = pltpu.VMEM((8, channels), F32)
    slots = pltpu.VMEM((n, 8, LANE), F32)
    one = pltpu.VMEM((8, LANE), F32)
    short_taps, filters, skip_bias = [
        pltpu.with_memory_space_constraint(x, pltpu.HBM) for x in (short_taps, filters, skip_bias)
    ]
    outs = pl.pallas_call(
        functools.partial(kernel, n, blocks),
        out_shape=(
            pltpu.VMEM(full, BF), pltpu.VMEM(full, BF), pltpu.VMEM(full, BF),
            row,
            pltpu.VMEM(short_taps.shape, F32),
            pltpu.VMEM(filters.shape, F32),
            pltpu.VMEM((1, LANE), F32),
        ),
        in_specs=[hbm] * 7,
        out_specs=(vmem,) * 7,
        scratch_shapes=[pltpu.VMEM(full, BF)] * 9
        + [
            pltpu.VMEM((3, channels, length), BF),
            pltpu.VMEM((3, 2, channels, length), BF),
            pltpu.VMEM((2, 2, blocks * GROUP, LANE), BF),
            pltpu.VMEM((2, 10, TILE, LANE), BF),
            pltpu.VMEM((2, 3, TILE, LANE), BF),
            pltpu.VMEM(tile, BF), pltpu.VMEM(tile, BF),
            pltpu.VMEM(tile, BF), pltpu.VMEM(tile, BF),
            pltpu.VMEM(short_taps.shape, F32),
            pltpu.VMEM(filters.shape, BF),
            pltpu.VMEM(skip_bias.shape, BF),
            pltpu.VMEM((9, channels, LANE), BF),
            pltpu.VMEM(tile, BF),
            row, row, row, row, one, slots, slots, slots, one, slots, row, row,
            dma((12,)), dma((2,)), dma((2,)),
            dma((CHUNKS,)), dma((CHUNKS,)), dma((CHUNKS,)), dma((CHUNKS,)),
            dma((2,)), dma((2,)), dma((2,)), dma((2,)),
        ],
        compiler_params=pltpu.CompilerParams(
            collective_id=0, has_side_effects=True, vmem_limit_bytes=48 * 1024 * 1024
        ),
    )(query_feat, key_feat, value_feat, grad_out, short_taps, filters, skip_bias)
    return pl.pallas_call(
        functools.partial(finish, blocks),
        out_shape=tuple(
            jax.ShapeDtypeStruct(s, d)
            for s, d in (
                (full, BF), (full, BF), (full, BF),
                (short_taps.shape, F32), (filters.shape, F32), (skip_bias.shape, F32),
            )
        ),
        in_specs=[vmem] * 7 + [hbm],
        out_specs=(hbm,) * 6,
        scratch_shapes=[
            pltpu.VMEM(short_taps.shape, F32),
            pltpu.VMEM((3,) + tile, BF),
            pltpu.VMEM(skip_bias.shape, F32),
            dma((7,)), dma((3,)),
        ],
        compiler_params=pltpu.CompilerParams(vmem_limit_bytes=16 * 1024 * 1024),
    )(*outs, short_taps)


def solution(mesh):
    wide, narrow = P("tp", "ctx"), P(None, None, "tp")
    both = ("tp", "ctx")

    def whole(*args):
        with jax.sharding.use_abstract_mesh(mesh.abstract_mesh):
            return jax.shard_map(
                body,
                mesh=mesh,
                in_specs=(wide, wide, wide, wide, narrow, P(both, None), P(both)),
                out_specs=(wide, wide, wide, narrow, P(both, None), P(both)),
                check_vma=False,
            )(*args)

    return whole
```
